32 devices in a mesh: wide: 8 (over y, x, core), grp: 4 (over z).
Axes of the slice: x: 2, y: 2, z: 4, core: 2. Of those that a mesh axis runs over, the one named last changes fastest.
Arguments:
- source: float32 [64, 64, 128], P('wide', 'grp'), may hold values from -6 to 6
- conductivity: float32 [64, 64, 128], P('wide', 'grp'), may hold values from 0.02 to 0.5
- ice_cells: int32 [64, 64], P('wide', 'grp'), may hold values from 1 to 128, as said below
Outputs:
- pressure: float32 [64, 64, 128], P('wide', 'grp')
The draws below stay inside these ranges and needn't reach their ends.
Inputs may be any that keep to these rules, and one draw needn't show every extreme that they name: Column (x, y) holds ice in its lowest ice_cells[x, y] cells; some column is 128 cells high.
All inputs are finite; a program needn't handle non-finite values.
Results may differ from the reference program's by a relative error of at most 0.0001.
Values sent between devices are 32-bit elements; how exact they have to be, the bound alone decides.
A program may use at most 64 MiB of HBM per device.

```python
import math
import jax
import jax.numpy as jnp

CZ = 128
ITERS = 6
NX = 64
NY = 64


def draw_source(key, part):
    values = jax.random.truncated_normal(key, -6.0, 6.0, (NX, NY, CZ), jnp.float32)
    return values


def draw_ice_cells(key, part):
    key_plateau = jax.random.fold_in(key, 11)
    key_rough = jax.random.fold_in(key, 12)
    key_summit = jax.random.fold_in(key, 13)
    plateau = jax.random.randint(key_plateau, (NX // 4, NY // 4), CZ // 8, CZ + 1)
    plateau = jnp.repeat(jnp.repeat(plateau, 4, 0), 4, 1)
    roughness = jax.random.randint(key_rough, (NX, NY), 0, CZ // 8 + 1)
    heights = jnp.clip(plateau - roughness, 1, CZ)
    summit = jax.random.randint(key_summit, (), 0, NX * NY)
    flattened = heights.reshape(-1)
    flattened = jnp.where(jnp.arange(NX * NY) == summit, CZ, flattened)
    return flattened.reshape(NX, NY).astype(jnp.int32)


def steps_of(stream_key, dims, split, low, top_value):
    level = 1.0
    for dim, blocks in split:
        steps = jax.random.uniform(jax.random.fold_in(jax.random.fold_in(stream_key, 6), dim), (blocks,), jnp.float32, low / len(split), top_value / len(split))
        level = level * jnp.repeat(jnp.exp(steps), dims[dim] // blocks).reshape((-1,) + (1,) * (len(dims) - 1 - dim))
    return level


def setup_inputs(seed: int = 0) -> dict:
    keys = jax.random.split(jax.random.key(seed), 4)
    source = draw_source(jax.random.fold_in(keys[3], 71), 0)
    conductivity = jnp.clip(jnp.exp(math.log(0.5) - 3.218876 * jax.random.uniform(keys[1], (NX, NY, CZ), jnp.float32) ** steps_of(keys[1], (NX, NY, CZ), ((0, 8), (1, 4)), -0.2, 0.2)), 0.02, 0.5)
    ice_cells = draw_ice_cells(jax.random.fold_in(keys[3], 71), 0)
    return dict(source=source, conductivity=conductivity, ice_cells=ice_cells)


cheb_center = (2.0 + 0.3) / 2.0
cheb_radius = (2.0 - 0.3) / 2.0
first_ratio = cheb_radius / cheb_center
second_ratio = 1.0 / (2.0 * cheb_center / cheb_radius - first_ratio)
carry_weight = second_ratio * first_ratio
fresh_weight = 2.0 * second_ratio / cheb_radius


def beside_all(values, above):
    padded = jnp.pad(values, ((1, 1), (1, 1), (0, 0)))
    below = jnp.zeros_like(above)
    return (padded[2:, 1:-1], padded[:-2, 1:-1], padded[1:-1, 2:], padded[1:-1, :-2],
            jnp.concatenate([values[:, :, 1:], above], 2),
            jnp.concatenate([below, values[:, :, :-1]], 2))


def level_setup(coef_field, heights, coarsening):
    factor = float(2 ** coarsening)
    others = beside_all(coef_field, coef_field[:, :, -1:])
    weights = tuple(factor * 2.0 * coef_field * neighbour / (coef_field + neighbour) for neighbour in others)
    diagonal = weights[0]
    for weight in weights[1:]:
        diagonal = diagonal + weight
    layers = jnp.arange(coef_field.shape[2], dtype=jnp.float32) * factor
    active = (layers[None, None, :] < heights[:, :, None]).astype(jnp.float32)
    return weights, diagonal, active


def operate(values, setup):
    weights, diagonal, active = setup
    others = beside_all(values, jnp.zeros_like(values[:, :, :1]))
    coupled = weights[0] * others[0]
    for weight, neighbour in zip(weights[1:], others[1:]):
        coupled = coupled + weight * neighbour
    return active * (diagonal * values - coupled)


def smooth(guess, source_term, setup, fresh):
    diagonal = setup[1]
    if fresh:
        residual = source_term
    else:
        residual = source_term - operate(guess, setup)
    update = residual / (cheb_center * diagonal)
    guess = update if fresh else guess + update
    residual = source_term - operate(guess, setup)
    update = carry_weight * update + fresh_weight * residual / diagonal
    return guess + update


def children_sum(values):
    extent_x, extent_y, extent_z = values.shape
    return values.reshape(extent_x // 2, 2, extent_y // 2, 2, extent_z // 2, 2).sum(axis=(1, 3, 5))


def column_top(heights):
    extent_x, extent_y = heights.shape
    return heights.reshape(extent_x // 2, 2, extent_y // 2, 2).max(axis=(1, 3))


def spread_children(values):
    return jnp.repeat(jnp.repeat(jnp.repeat(values, 2, 0), 2, 1), 2, 2)


def conjugate(source_term, setup):
    solution = jnp.zeros_like(source_term)
    residual = source_term
    direction = source_term
    current = jnp.sum(residual * residual)
    for iteration in range(ITERS):
        applied = operate(direction, setup)
        step_size = current / jnp.sum(direction * applied)
        solution = solution + step_size * direction
        residual = residual - step_size * applied
        following = jnp.sum(residual * residual)
        direction = residual + (following / current) * direction
        current = following
    return solution


def reference(source, conductivity, ice_cells):
    heights = ice_cells.astype(jnp.float32)
    setup_fine = level_setup(conductivity, heights, 0)
    load_fine = setup_fine[2] * source
    smooth_fine = smooth(jnp.zeros_like(load_fine), load_fine, setup_fine, True)
    load_middle = children_sum(load_fine - operate(smooth_fine, setup_fine))
    coef_middle = children_sum(conductivity) * 0.125
    heights_middle = column_top(heights)
    setup_middle = level_setup(coef_middle, heights_middle, 1)
    smooth_middle = smooth(jnp.zeros_like(load_middle), load_middle, setup_middle, True)
    load_coarse = children_sum(load_middle - operate(smooth_middle, setup_middle))
    coef_coarse = children_sum(coef_middle) * 0.125
    setup_coarse = level_setup(coef_coarse, column_top(heights_middle), 2)
    coarse = conjugate(load_coarse, setup_coarse)
    smooth_middle = smooth_middle + setup_middle[2] * spread_children(coarse)
    smooth_middle = smooth(smooth_middle, load_middle, setup_middle, False)
    smooth_fine = smooth_fine + setup_fine[2] * spread_children(smooth_middle)
    return smooth(smooth_fine, load_fine, setup_fine, False)
```

```python
import jax
import jax.numpy as jnp
from jax import lax
from jax.experimental import pallas as pl
from jax.experimental.pallas import tpu as pltpu
from jax.sharding import PartitionSpec as P

ITERS = 6
HALO = 8
TINY = 1e-30

cheb_center = (2.0 + 0.3) / 2.0
cheb_radius = (2.0 - 0.3) / 2.0
first_ratio = cheb_radius / cheb_center
second_ratio = 1.0 / (2.0 * cheb_center / cheb_radius - first_ratio)
carry_weight = second_ratio * first_ratio
fresh_weight = 2.0 * second_ratio / cheb_radius

DIRECTIONS = [(dx, dy) for dx in (-1, 0, 1) for dy in (-1, 0, 1) if (dx, dy) != (0, 0)]


def planes(low, high, body, carry=None):
    count = high - low
    unroll = count if count <= 32 else 4
    if carry is None:

        def step(x, _):
            body(x)
            return 0

        lax.fori_loop(low, high, step, 0, unroll=unroll)
        return None
    return lax.fori_loop(low, high, body, carry, unroll=unroll)


class Level:
    def __init__(self, count, width, depth, rep, wx, yp, ym, zp, zm, diag, inv, act):
        self.count, self.width, self.depth, self.rep = count, width, depth, rep
        self.wx, self.yp, self.ym, self.zp, self.zm = wx, yp, ym, zp, zm
        self.diag, self.inv, self.act = diag, inv, act

    def setup(self, coef, top):
        factor = float(self.rep)
        width, depth, rep = self.width, self.depth, self.rep
        lane = lax.broadcasted_iota(jnp.int32, (width, depth), 1)
        row = lax.broadcasted_iota(jnp.int32, (width, depth), 0)
        last_lane = lane >= depth - rep
        last_row = row == width - 1
        layer = ((lane // rep) * rep).astype(jnp.float32)

        def face(c, n):
            return factor * 2.0 * c * n / (c + n + TINY)

        self.wx[0] = jnp.zeros((width, depth), jnp.float32)

        def body(x):
            c = coef(x)
            plus_x = face(c, coef(x + 1))
            self.wx[x + 1] = plus_x
            plus_y = face(c, jnp.where(last_row, 0.0, pltpu.roll(c, width - 1, 0)))
            plus_z = face(c, jnp.where(last_lane, 0.0, pltpu.roll(c, depth - rep, 1)))
            minus_y = pltpu.roll(plus_y, 1, 0)
            minus_z = pltpu.roll(plus_z, rep, 1)
            above = jnp.where(last_lane, factor * c, plus_z)
            diag = plus_x + self.wx[x] + plus_y + minus_y + above + minus_z
            self.yp[x] = plus_y
            self.ym[x] = minus_y
            self.zp[x] = plus_z
            self.zm[x] = minus_z
            self.diag[x] = diag
            self.inv[x] = 1.0 / jnp.maximum(diag, TINY)
            self.act[x] = (layer < top(x)).astype(jnp.float32)

        planes(0, self.count, body)

    def apply(self, v, x):
        here = v[x + 1]
        coupled = self.wx[x + 1] * v[x + 2] + self.wx[x] * v[x]
        coupled = coupled + self.yp[x] * pltpu.roll(here, self.width - 1, 0)
        coupled = coupled + self.ym[x] * pltpu.roll(here, 1, 0)
        coupled = coupled + self.zp[x] * pltpu.roll(here, self.depth - self.rep, 1)
        coupled = coupled + self.zm[x] * pltpu.roll(here, self.rep, 1)
        return self.act[x] * (self.diag[x] * here - coupled)

    def smooth_fresh(self, f, u, out):
        def first(x):
            u[x + 1] = f[x] * self.inv[x] * (1.0 / cheb_center)

        planes(0, self.count, first)

        def second(x):
            residual = f[x] - self.apply(u, x)
            before = u[x + 1]
            update = carry_weight * before + fresh_weight * (residual * self.inv[x])
            out[x + 1] = before + update

        planes(0, self.count, second)

    def smooth_again(self, guess, f, e, u, low, high, put):
        def first(x):
            residual = f[x] - self.apply(guess, x)
            update = residual * self.inv[x] * (1.0 / cheb_center)
            e[x] = update
            u[x + 1] = guess[x + 1] + update

        planes(low - 1, high + 1, first)

        def second(x):
            residual = f[x] - self.apply(u, x)
            update = carry_weight * e[x] + fresh_weight * (residual * self.inv[x])
            put(x, u[x + 1] + update)

        planes(low, high, second)


def pair_lanes(values, rep, join):
    width, depth = values.shape
    lane = lax.broadcasted_iota(jnp.int32, (width, depth), 1)
    lower = (lane // rep) % 2 == 0
    partner = jnp.where(lower, pltpu.roll(values, depth - rep, 1), pltpu.roll(values, rep, 1))
    return join(values, partner)


def pair_rows(values, buffer, x, join):
    half = values.shape[0] // 2
    buffer[x] = values
    return join(buffer[x, pl.ds(0, half, stride=2)], buffer[x, pl.ds(1, half, stride=2)])


def keep_lane(values, slot, slots):
    width, depth = values.shape
    lane = lax.broadcasted_iota(jnp.int32, (width, depth), 1)
    kept = jnp.where(lane % slots == slot, values, 0.0)
    if slot:
        kept = pltpu.roll(kept, depth - slot, 1)
    shift = 1
    while shift < slots:
        kept = kept + pltpu.roll(kept, shift, 1)
        shift *= 2
    return kept


def add(a, b):
    return a + b


def kernel(wide, grp, source, conductivity, ice, out, *scratch):
    (fine, fw, f_load, f_u, f_smooth, f_e, pool_a, pool_b, pool_c,
     m_load, m_coef, m_top, mw, m_u, m_smooth, packed,
     outer, o_load, o_coef, o_top, ow, o_u, o_smooth, o_e, o_corr,
     pool_d, pool_e, pool_f, mine, gathered, g_coef, g_top, gw, g_x, g_r, g_d, g_a,
     spread, send_a, recv_a, send_b, recv_b, send_c, recv_c) = scratch
    bx, by, depth = source.shape
    bx1, by1, bx2, by2 = bx // 2, by // 2, bx // 4, by // 4
    x0, y0 = bx + 2 * HALO, by + 2 * HALO
    x1, y1 = x0 // 2, y0 // 2
    ring = bx1 + 1
    xo, yo = bx1 + 2 * ring, 3 * by1
    nx2, ny2 = wide * bx2, grp * by2
    w, g = lax.axis_index("wide"), lax.axis_index("grp")
    peers = wide * grp
    me = w * grp + g

    def clear(ref):
        def body(x):
            ref[x] = jnp.zeros(ref.shape[1:], ref.dtype)

        planes(0, ref.shape[0], body)

    for channel in range(3):
        clear(fine.at[channel])
    for channel in range(2):
        clear(outer.at[channel])

    barrier = pltpu.get_barrier_semaphore()

    def greet(d, _):
        other = lax.rem(me + d, peers)
        pl.semaphore_signal(barrier, inc=1, device_id=(other // grp, lax.rem(other, grp)),
                            device_id_type=pl.DeviceIdType.MESH)
        return 0

    lax.fori_loop(1, peers, greet, 0)

    rows16 = lax.broadcasted_iota(jnp.int32, (by, by), 0)
    cols16 = lax.broadcasted_iota(jnp.int32, (by, by), 1)
    eye = (rows16 == cols16).astype(jnp.float32)
    heights = ice[...].astype(jnp.float32)
    for x in range(bx):
        fine[0, HALO + x + 1, HALO:HALO + by] = source[x]
        fine[1, HALO + x + 1, HALO:HALO + by] = conductivity[x]
        column = jnp.sum(eye * heights[x:x + 1], axis=1, keepdims=True)
        fine[2, HALO + x + 1, HALO:HALO + by] = jnp.broadcast_to(column, (by, depth))
    for ref in (f_u, f_smooth, m_u, m_smooth, o_u, o_smooth, o_corr, g_d):
        ref[0] = jnp.zeros(ref.shape[1:], jnp.float32)
        ref[ref.shape[0] - 1] = jnp.zeros(ref.shape[1:], jnp.float32)
    for ref in (m_coef, o_coef, g_coef):
        ref[0] = jnp.zeros(ref.shape[1:], jnp.float32)
        ref[ref.shape[0] - 1] = jnp.zeros(ref.shape[1:], jnp.float32)
    clear_x = g_x.shape[0]
    for k in range(grp + 2):
        def blank(x):
            g_x[x, k] = jnp.zeros((by2, depth), jnp.float32)
        planes(0, clear_x, blank)

    pl.semaphore_wait(barrier, peers - 1)

    def inside(dx, dy):
        return (w + dx >= 0) & (w + dx < wide) & (g + dy >= 0) & (g + dy < grp)

    def copy_fine(k, dx, dy):
        src_x, dst_x, len_x = {
            1: (1 + bx, 1, HALO), 0: (1 + HALO, 1 + HALO, bx), -1: (1 + HALO, 1 + HALO + bx, HALO)
        }[dx]
        src_y, dst_y, len_y = {
            1: (by, 0, HALO), 0: (HALO, HALO, by), -1: (HALO, HALO + by, HALO)
        }[dy]
        return pltpu.make_async_remote_copy(
            src_ref=fine.at[:, pl.ds(src_x, len_x), pl.ds(src_y, len_y)],
            dst_ref=fine.at[:, pl.ds(dst_x, len_x), pl.ds(dst_y, len_y)],
            send_sem=send_a.at[k], recv_sem=recv_a.at[k],
            device_id=(w + dx, g + dy), device_id_type=pl.DeviceIdType.MESH)

    def copy_outer(k, dx, dy):
        src_x, dst_x, len_x = {
            1: (0, 0, ring), 0: (1, ring, bx1), -1: (1, ring + bx1, ring)
        }[dx]
        dst_y = {1: 0, 0: by1, -1: 2 * by1}[dy]
        return pltpu.make_async_remote_copy(
            src_ref=packed.at[:, pl.ds(src_x, len_x)],
            dst_ref=outer.at[:, pl.ds(dst_x, len_x), pl.ds(dst_y, by1)],
            send_sem=send_b.at[k], recv_sem=recv_b.at[k],
            device_id=(w + dx, g + dy), device_id_type=pl.DeviceIdType.MESH)

    def all_directions(make, sign, act):
        for k, (dx, dy) in enumerate(DIRECTIONS):
            @pl.when(inside(sign * dx, sign * dy))
            def _():
                act(make(k, dx, dy))

    all_directions(copy_fine, 1, lambda c: c.start())
    all_directions(copy_fine, -1, lambda c: c.wait_recv())

    level0 = Level(x0, y0, depth, 1, *fw)
    level0.setup(lambda x: fine[1, x + 1], lambda x: fine[2, x + 1])

    def load0(x):
        f_load[x] = level0.act[x] * fine[0, x + 1]

    planes(0, x0, load0)
    level0.smooth_fresh(f_load, f_u, f_smooth)

    def restrict0(x):
        a, b = 2 * x, 2 * x + 1
        rest = (f_load[a] - level0.apply(f_smooth, a)) + (f_load[b] - level0.apply(f_smooth, b))
        m_load[x] = pair_rows(pair_lanes(rest, 1, add), pool_a, x, add)
        coef = fine[1, a + 1] + fine[1, b + 1]
        m_coef[x + 1] = pair_rows(pair_lanes(coef, 1, add), pool_b, x, add) * 0.125
        top = jnp.maximum(fine[2, a + 1], fine[2, b + 1])
        m_top[x] = pair_rows(top, pool_c, x, jnp.maximum)

    planes(0, x1, restrict0)

    half = HALO // 2
    even = lax.broadcasted_iota(jnp.int32, (by1, depth), 1) % 2 == 0
    for r in range(bx1 + 2):
        x = half - 1 + r
        packed[0, r] = jnp.where(even, m_load[x, half:half + by1], m_coef[x + 1, half:half + by1])
        packed[1, r] = m_top[x, half:half + by1]
    all_directions(copy_outer, 1, lambda c: c.start())
    for r in range(bx1):
        for channel in range(2):
            outer[channel, ring + r, by1:2 * by1] = packed[channel, r + 1]

    level1 = Level(x1, y1, depth, 2, *mw)
    level1.setup(lambda x: m_coef[x + 1], lambda x: m_top[x])
    level1.smooth_fresh(m_load, m_u, m_smooth)
    quarter = half // 2
    slot = lax.broadcasted_iota(jnp.int32, (by2, depth), 1) % 4
    for x in range(bx2):
        a, b = half + 2 * x, half + 2 * x + 1
        rest = (m_load[a] - level1.apply(m_smooth, a)) + (m_load[b] - level1.apply(m_smooth, b))
        load = pair_rows(pair_lanes(rest, 2, add), pool_d, x, add)
        coef = pair_rows(pair_lanes(m_coef[a + 1] + m_coef[b + 1], 2, add), pool_e, x, add) * 0.125
        top = pair_rows(jnp.maximum(m_top[a], m_top[b]), pool_f, x, jnp.maximum)
        load, coef, top = (v[quarter:quarter + by2] for v in (load, coef, top))
        mine[x] = jnp.where(slot == 0, load, jnp.where(slot == 1, coef, top))

    def copy_coarse(d, from_w, from_g, to):
        return pltpu.make_async_remote_copy(
            src_ref=mine, dst_ref=gathered.at[from_g, pl.ds(from_w * bx2, bx2)],
            send_sem=send_c.at[d], recv_sem=recv_c.at[d],
            device_id=(to // grp, lax.rem(to, grp)), device_id_type=pl.DeviceIdType.MESH)

    def give(d, _):
        copy_coarse(d, w, g, lax.rem(me + d, peers)).start()
        return 0

    lax.fori_loop(1, peers, give, 0)
    for x in range(bx2):
        gathered[g, w * bx2 + x] = mine[x]

    all_directions(copy_outer, -1, lambda c: c.wait_recv())

    def unpack1(x):
        both = outer[0, x]
        o_load[x] = keep_lane(both, 0, 2)
        o_coef[x + 1] = keep_lane(both, 1, 2)

    planes(0, xo, unpack1)
    level_o = Level(xo, yo, depth, 2, *ow)
    level_o.setup(lambda x: o_coef[x + 1], lambda x: outer[1, x])
    level_o.smooth_fresh(o_load, o_u, o_smooth)

    def take(d, _):
        source_of = lax.rem(me + peers - d, peers)
        copy_coarse(d, source_of // grp, lax.rem(source_of, grp), me).wait_recv()
        return 0

    lax.fori_loop(1, peers, take, 0)

    def unpack2(x):
        for k in range(grp):
            g_a[x, k * by2:(k + 1) * by2] = gathered[k, x]
        everything = g_a[x]
        load = keep_lane(everything, 0, 4)
        g_r[x] = load
        g_d[x + 1] = load
        g_coef[x + 1] = keep_lane(everything, 1, 4)
        g_top[x] = keep_lane(everything, 2, 4)

    planes(0, nx2, unpack2)
    level2 = Level(nx2, ny2, depth, 4, *gw)
    level2.setup(lambda x: g_coef[x + 1], lambda x: g_top[x])
    zero = jnp.zeros((ny2, depth), jnp.float32)

    def total(values):
        return jnp.sum(values, axis=(0, 1), keepdims=True)

    current = total(planes(0, nx2, lambda x, acc: acc + g_r[x] * g_r[x], zero))
    sol = ow_sol = spread[1]

    def first_sol(x):
        sol[x] = zero

    planes(0, nx2, first_sol)

    def iterate(_, current):
        def image(x, acc):
            applied = level2.apply(g_d, x)
            g_a[x] = applied
            return acc + g_d[x + 1] * applied

        step = current / total(planes(0, nx2, image, zero))

        def move(x, acc):
            sol[x] = sol[x] + step * g_d[x + 1]
            residual = g_r[x] - step * g_a[x]
            g_r[x] = residual
            return acc + residual * residual

        following = total(planes(0, nx2, move, zero))
        ratio = following / current

        def turn(x):
            g_d[x + 1] = g_r[x] + ratio * g_d[x + 1]

        planes(0, nx2, turn)
        return following

    lax.fori_loop(0, ITERS, iterate, current)

    pad = 3

    def cut(x):
        for k in range(grp):
            g_x[x + pad, k + 1] = sol[x, k * by2:(k + 1) * by2]

    planes(0, nx2, cut)

    wide_rows = spread[0]
    for x in range(xo):
        parent = (x - ring) // 2
        for k in range(3):
            piece = g_x[w * bx2 + parent + pad, g + k]
            wide_rows[x, pl.ds(k * by1, by2, stride=2)] = piece
            wide_rows[x, pl.ds(k * by1 + 1, by2, stride=2)] = piece
        o_corr[x + 1] = o_smooth[x + 1] + level_o.act[x] * wide_rows[x]

    def put_outer(x, value):
        o_load[x] = value

    level_o.smooth_again(o_corr, o_load, o_e, o_u, ring - 1, ring + bx1 + 1, put_outer)

    fine_rows = spread[2]
    for x in range(HALO - 2, HALO + bx + 2):
        parent = o_load[(x - HALO) // 2 + ring, by1 - half:2 * by1 + half]
        fine_rows[x, pl.ds(0, y1, stride=2)] = parent
        fine_rows[x, pl.ds(1, y1, stride=2)] = parent
        f_smooth[x + 1] = f_smooth[x + 1] + level0.act[x] * fine_rows[x]

    def put_fine(x, value):
        out[x - HALO] = value[HALO:HALO + by]

    level0.smooth_again(f_smooth, f_load, f_e, f_u, HALO, HALO + bx, put_fine)

    all_directions(copy_fine, 1, lambda c: c.wait_send())
    all_directions(copy_outer, 1, lambda c: c.wait_send())

    def given(d, _):
        copy_coarse(d, w, g, lax.rem(me + d, peers)).wait_send()
        return 0

    lax.fori_loop(1, peers, given, 0)


def shards(source, conductivity, ice_cells):
    wide, grp = lax.axis_size("wide"), lax.axis_size("grp")
    bx, by, depth = source.shape
    bx1, by1, bx2, by2 = bx // 2, by // 2, bx // 4, by // 4
    x0, y0 = bx + 2 * HALO, by + 2 * HALO
    x1, y1 = x0 // 2, y0 // 2
    ring = bx1 + 1
    xo, yo = bx1 + 2 * ring, 3 * by1
    nx2, ny2 = wide * bx2, grp * by2
    peers = wide * grp

    def block(*shape):
        return pltpu.VMEM(shape + (depth,), jnp.float32)

    def held(count, width):
        return [block(count + 1, width)] + [block(count, width) for _ in range(7)]

    dma = pltpu.SemaphoreType.DMA
    scratch = [
        block(3, x0 + 2, y0), held(x0, y0), block(x0, y0), block(x0 + 2, y0), block(x0 + 2, y0),
        block(x0, y0), block(x1, y0), block(x1, y0), block(x1, y0),
        block(x1, y1), block(x1 + 2, y1), block(x1, y1), held(x1, y1), block(x1 + 2, y1),
        block(x1 + 2, y1), block(2, bx1 + 2, by1),
        block(2, xo, yo), block(xo, yo), block(xo + 2, yo), block(xo, yo), held(xo, yo),
        block(xo + 2, yo), block(xo + 2, yo), block(xo, yo), block(xo + 2, yo),
        block(bx2, y1), block(bx2, y1), block(bx2, y1), block(bx2, by2),
        block(grp, nx2, by2), block(nx2 + 2, ny2), block(nx2, ny2), held(nx2, ny2),
        block(nx2 + 6, grp + 2, by2), block(nx2, ny2), block(nx2 + 2, ny2), block(nx2, ny2),
        [block(xo, yo), block(nx2, ny2), block(x0, y0)],
        dma((8,)), dma((8,)), dma((8,)), dma((8,)), dma((peers,)), dma((peers,)),
    ]
    leaves, tree = jax.tree.flatten(scratch)

    def body(source_ref, conductivity_ref, ice_ref, out_ref, *refs):
        kernel(wide, grp, source_ref, conductivity_ref, ice_ref, out_ref,
               *jax.tree.unflatten(tree, refs))

    vmem = pl.BlockSpec(memory_space=pltpu.VMEM)
    return pl.pallas_call(
        body,
        out_shape=jax.ShapeDtypeStruct(source.shape, source.dtype),
        in_specs=[vmem] * 3,
        out_specs=vmem,
        scratch_shapes=leaves,
        compiler_params=pltpu.CompilerParams(
            collective_id=0, has_side_effects=True, vmem_limit_bytes=48 * 1024 * 1024
        ),
    )(source, conductivity, ice_cells)


def solution(mesh):
    placed = (P("wide", "grp", None), P("wide", "grp", None), P("wide", "grp"))
    return jax.shard_map(
        shards, mesh=mesh, in_specs=placed, out_specs=P("wide", "grp", None), check_vma=False
    )
```

```python
import jax
import jax.numpy as jnp
from jax import lax
from jax.experimental import pallas as pl
from jax.experimental.pallas import tpu as pltpu
from jax.sharding import PartitionSpec as P

ITERS = 6
HALO = 8
TINY = 1e-30

cheb_center = (2.0 + 0.3) / 2.0
cheb_radius = (2.0 - 0.3) / 2.0
first_ratio = cheb_radius / cheb_center
second_ratio = 1.0 / (2.0 * cheb_center / cheb_radius - first_ratio)
carry_weight = second_ratio * first_ratio
fresh_weight = 2.0 * second_ratio / cheb_radius

DIRECTIONS = [(dx, dy) for dx in (-1, 0, 1) for dy in (-1, 0, 1) if (dx, dy) != (0, 0)]


def planes(low, high, body, carry=None):
    count = high - low
    unroll = count if count <= 32 else 4
    if carry is None:

        def step(x, _):
            body(x)
            return 0

        lax.fori_loop(low, high, step, 0, unroll=unroll)
        return None
    return lax.fori_loop(low, high, body, carry, unroll=unroll)


class Level:
    def __init__(self, count, width, depth, rep, wx, yp, ym, zp, zm, diag, inv, act):
        self.count, self.width, self.depth, self.rep = count, width, depth, rep
        self.wx, self.yp, self.ym, self.zp, self.zm = wx, yp, ym, zp, zm
        self.diag, self.inv, self.act = diag, inv, act

    def setup(self, coef, top, low, high):
        factor = float(self.rep)
        width, depth, rep = self.width, self.depth, self.rep
        lane = lax.broadcasted_iota(jnp.int32, (width, depth), 1)
        row = lax.broadcasted_iota(jnp.int32, (width, depth), 0)
        last_lane = lane >= depth - rep
        last_row = row == width - 1
        layer = ((lane // rep) * rep).astype(jnp.float32)

        def face(c, n):
            return factor * 2.0 * c * n / (c + n + TINY)

        self.wx[low] = face(coef(low), coef(low - 1))

        def body(x):
            c = coef(x)
            plus_x = face(c, coef(x + 1))
            self.wx[x + 1] = plus_x
            plus_y = face(c, jnp.where(last_row, 0.0, pltpu.roll(c, width - 1, 0)))
            plus_z = face(c, jnp.where(last_lane, 0.0, pltpu.roll(c, depth - rep, 1)))
            minus_y = pltpu.roll(plus_y, 1, 0)
            minus_z = pltpu.roll(plus_z, rep, 1)
            above = jnp.where(last_lane, factor * c, plus_z)
            diag = plus_x + self.wx[x] + plus_y + minus_y + above + minus_z
            self.yp[x] = plus_y
            self.ym[x] = minus_y
            self.zp[x] = plus_z
            self.zm[x] = minus_z
            self.diag[x] = diag
            self.inv[x] = 1.0 / jnp.maximum(diag, TINY)
            self.act[x] = (layer < top(x)).astype(jnp.float32)

        planes(low, high, body)

    def apply(self, v, x):
        here = v[x + 1]
        coupled = self.wx[x + 1] * v[x + 2] + self.wx[x] * v[x]
        coupled = coupled + self.yp[x] * pltpu.roll(here, self.width - 1, 0)
        coupled = coupled + self.ym[x] * pltpu.roll(here, 1, 0)
        coupled = coupled + self.zp[x] * pltpu.roll(here, self.depth - self.rep, 1)
        coupled = coupled + self.zm[x] * pltpu.roll(here, self.rep, 1)
        return self.act[x] * (self.diag[x] * here - coupled)

    def smooth_fresh(self, f, u, out, low, high):
        def first(x):
            u[x + 1] = f[x] * self.inv[x] * (1.0 / cheb_center)

        planes(low, high, first)
        low, high = (low + 1, high - 1) if low else (low, high)

        def second(x):
            residual = f[x] - self.apply(u, x)
            before = u[x + 1]
            update = carry_weight * before + fresh_weight * (residual * self.inv[x])
            out[x + 1] = before + update

        planes(low, high, second)

    def smooth_again(self, guess, f, e, u, low, high, put):
        def first(x):
            residual = f[x] - self.apply(guess, x)
            update = residual * self.inv[x] * (1.0 / cheb_center)
            e[x] = update
            u[x + 1] = guess[x + 1] + update

        planes(low - 1, high + 1, first)

        def second(x):
            residual = f[x] - self.apply(u, x)
            update = carry_weight * e[x] + fresh_weight * (residual * self.inv[x])
            put(x, u[x + 1] + update)

        planes(low, high, second)


def pair_lanes(values, rep, join):
    width, depth = values.shape
    lane = lax.broadcasted_iota(jnp.int32, (width, depth), 1)
    lower = (lane // rep) % 2 == 0
    partner = jnp.where(lower, pltpu.roll(values, depth - rep, 1), pltpu.roll(values, rep, 1))
    return join(values, partner)


def pair_rows(values, buffer, x, join):
    half = values.shape[0] // 2
    buffer[x] = values
    return join(buffer[x, pl.ds(0, half, stride=2)], buffer[x, pl.ds(1, half, stride=2)])


def keep_lane(values, slot, slots):
    width, depth = values.shape
    lane = lax.broadcasted_iota(jnp.int32, (width, depth), 1)
    kept = jnp.where(lane % slots == slot, values, 0.0)
    if slot:
        kept = pltpu.roll(kept, depth - slot, 1)
    shift = 1
    while shift < slots:
        kept = kept + pltpu.roll(kept, shift, 1)
        shift *= 2
    return kept


def add(a, b):
    return a + b


def selector(count, first, stride, depth):
    rows = lax.broadcasted_iota(jnp.int32, (count, depth), 0)
    lanes = lax.broadcasted_iota(jnp.int32, (count, depth), 1)
    return (lanes == rows * stride + first).astype(jnp.float32)


def column(pick, row):
    return jnp.broadcast_to(jnp.sum(pick * row, axis=1, keepdims=True), pick.shape)


def kernel(wide, grp, source, conductivity, ice, out, *scratch):
    (fine, fw, f_load, f_u, f_smooth, f_e, f_top, pool_a, pool_b,
     m_load, m_coef, mw, m_u, m_smooth, packed,
     outer, o_load, o_coef, o_top, ow, o_u, o_smooth, o_e, o_corr,
     pool_d, pool_g, pool_h, mine, mine_c, gathered, gathered_c,
     g_coef, g_top, gw, g_x, g_r, g_d, g_a,
     spread, tops, ice_here, sem_in,
     send_a, recv_a, send_t, recv_t, send_s, recv_s, send_b, recv_b,
     send_c, recv_c, send_g, recv_g) = scratch
    bx, by, depth = source.shape
    bx1, by1, bx2, by2 = bx // 2, by // 2, bx // 4, by // 4
    x0, y0 = bx + 2 * HALO, by + 2 * HALO
    x1, y1 = x0 // 2, y0 // 2
    ring = bx1 + 1
    xo, yo = bx1 + 2 * ring, 3 * by1
    nx2, ny2 = wide * bx2, grp * by2
    half, quarter = HALO // 2, HALO // 4
    w, g = lax.axis_index("wide"), lax.axis_index("grp")
    peers = wide * grp
    me = w * grp + g

    middle = (pl.ds(HALO + 1, bx), pl.ds(HALO, by))
    load_source = pltpu.make_async_copy(source, fine.at[(0,) + middle], sem_in.at[0])
    load_coef = pltpu.make_async_copy(conductivity, fine.at[(1,) + middle], sem_in.at[1])
    load_ice = pltpu.make_async_copy(ice, ice_here, sem_in.at[2])
    load_ice.start()
    load_coef.start()
    load_source.start()

    for channel in range(2):
        for x in range(x0 + 2):
            if HALO < x <= HALO + bx:
                fine[channel, x, 0:HALO] = jnp.zeros((HALO, depth), jnp.float32)
                fine[channel, x, HALO + by:y0] = jnp.zeros((HALO, depth), jnp.float32)
            else:
                fine[channel, x] = jnp.zeros((y0, depth), jnp.float32)

    def clear(ref):
        def body(x):
            ref[x] = jnp.zeros(ref.shape[1:], ref.dtype)

        planes(0, ref.shape[0], body)

    clear(outer)
    clear(tops)

    barrier = pltpu.get_barrier_semaphore()

    def mesh_id(other):
        return (other // grp, lax.rem(other, grp))

    def greet(d, _):
        pl.semaphore_signal(barrier, inc=1, device_id=mesh_id(lax.rem(me + d, peers)),
                            device_id_type=pl.DeviceIdType.MESH)
        return 0

    lax.fori_loop(1, peers, greet, 0)

    for ref in (f_u, f_smooth, m_u, m_smooth, o_u, o_smooth, o_corr, g_d, m_coef, o_coef, g_coef):
        ref[0] = jnp.zeros(ref.shape[1:], jnp.float32)
        ref[ref.shape[0] - 1] = jnp.zeros(ref.shape[1:], jnp.float32)
    clear(g_x)

    load_ice.wait()
    tops[4, :, 0:by] = ice_here[...].astype(jnp.float32)
    load_coef.wait()
    slot = lax.broadcasted_iota(jnp.int32, (by2, depth), 1)
    sub = lax.broadcasted_iota(jnp.int32, (by2, depth), 0)
    chosen = slot % 4 == sub
    pick2 = selector(by2, 0, 4, depth)

    def fold(values):
        return jnp.sum(jnp.where(chosen, values, 0.0), axis=0, keepdims=True)

    all_tops = jnp.zeros((1, depth), jnp.float32)
    for x in range(bx2):
        coef = None
        for r in range(2):
            a = HALO + 1 + 4 * x + 2 * r
            pair = fine[1, a, HALO:HALO + by] + fine[1, a + 1, HALO:HALO + by]
            pair = pair_rows(pair_lanes(pair, 1, add), pool_g, 2 * x + r, add) * 0.125
            coef = pair if coef is None else coef + pair
        coef = pair_rows(pair_lanes(coef, 2, add), pool_h, x, add) * 0.125
        mine_c[x:x + 1] = fold(coef)
        top = jnp.max(tops[4, 4 * x:4 * x + 4], axis=0, keepdims=True)
        top = jnp.maximum(top, pltpu.roll(top, depth - 1, 1))
        top = jnp.maximum(top, pltpu.roll(top, depth - 2, 1))
        spot = slot // (depth // bx2) == x
        all_tops = all_tops + fold(jnp.where(spot, column(pick2, top), 0.0))
    mine_c[bx2:bx2 + 1] = all_tops

    load_source.wait()
    pl.semaphore_wait(barrier, peers - 1)

    def inside(dx, dy):
        return (w + dx >= 0) & (w + dx < wide) & (g + dy >= 0) & (g + dy < grp)

    def remote(src, dst, send, recv, device):
        return pltpu.make_async_remote_copy(
            src_ref=src, dst_ref=dst, send_sem=send, recv_sem=recv,
            device_id=device, device_id_type=pl.DeviceIdType.MESH)

    def copy_fine(channel, send, recv):
        def make(k, dx, dy):
            rows = HALO - 1 if dy == 0 else HALO - 2
            src_x, dst_x, len_x = {
                1: (1 + HALO + bx - rows, 1 + HALO - rows, rows),
                0: (1 + HALO, 1 + HALO, bx),
                -1: (1 + HALO, 1 + HALO + bx, rows),
            }[dx]
            src_y, dst_y, len_y = {
                1: (by, 0, HALO), 0: (HALO, HALO, by), -1: (HALO, HALO + by, HALO)
            }[dy]
            return remote(
                fine.at[channel, pl.ds(src_x, len_x), pl.ds(src_y, len_y)],
                fine.at[channel, pl.ds(dst_x, len_x), pl.ds(dst_y, len_y)],
                send.at[k], recv.at[k], (w + dx, g + dy))

        return make

    copy_coef = copy_fine(1, send_a, recv_a)
    copy_source = copy_fine(0, send_s, recv_s)

    def copy_tops(k, dx, dy):
        return remote(tops.at[4], tops.at[(1 - dx) * 3 + 1 - dy],
                      send_t.at[k], recv_t.at[k], (w + dx, g + dy))

    def copy_outer(k, dx, dy):
        src_x, dst_x, len_x = {
            1: (0, 0, ring), 0: (1, ring, bx1), -1: (1, ring + bx1, ring)
        }[dx]
        dst_y = {1: 0, 0: by1, -1: 2 * by1}[dy]
        return remote(packed.at[pl.ds(src_x, len_x)],
                      outer.at[pl.ds(dst_x, len_x), pl.ds(dst_y, by1)],
                      send_b.at[k], recv_b.at[k], (w + dx, g + dy))

    def all_directions(make, sign, act):
        for k, (dx, dy) in enumerate(DIRECTIONS):
            @pl.when(inside(sign * dx, sign * dy))
            def _():
                act(make(k, dx, dy))

    def copy_all(block, places, send, recv):
        def make(d, owner, to):
            return remote(block, places.at[owner], send.at[d], recv.at[d], mesh_id(to))

        def start():
            def body(d, _):
                make(d, me, lax.rem(me + d, peers)).start()
                return 0
            lax.fori_loop(1, peers, body, 0)

        def arrived():
            def body(d, _):
                make(d, lax.rem(me + peers - d, peers), me).wait_recv()
                return 0
            lax.fori_loop(1, peers, body, 0)

        def sent():
            def body(d, _):
                make(d, me, lax.rem(me + d, peers)).wait_send()
                return 0
            lax.fori_loop(1, peers, body, 0)

        return start, arrived, sent

    coarse_start, coarse_arrived, coarse_sent = copy_all(mine, gathered, send_c, recv_c)
    consts_start, consts_arrived, consts_sent = copy_all(mine_c, gathered_c, send_g, recv_g)

    all_directions(copy_coef, 1, lambda c: c.start())
    all_directions(copy_tops, 1, lambda c: c.start())
    all_directions(copy_source, 1, lambda c: c.start())
    consts_start()
    gathered_c[me] = mine_c[...]

    all_directions(copy_tops, -1, lambda c: c.wait_recv())
    reach = HALO - 2
    picks = (selector(HALO, by - HALO, 1, depth), selector(by, 0, 1, depth),
             selector(HALO, 0, 1, depth))
    starts = (0, HALO, HALO + by)
    for x in range(HALO - reach, HALO + bx + reach):
        row = x - HALO + bx
        for k in range(3):
            line = tops[row // bx * 3 + k, row % bx:row % bx + 1]
            f_top[x, starts[k]:starts[k] + picks[k].shape[0]] = column(picks[k], line)
    pick1 = selector(by1, 0, 2, depth)
    for x in range(1, xo - 1):
        row = 2 * (x - 1)
        for k in range(3):
            line = jnp.max(tops[row // bx * 3 + k, row % bx:row % bx + 2], axis=0, keepdims=True)
            line = jnp.maximum(line, pltpu.roll(line, depth - 1, 1))
            o_top[x, k * by1:(k + 1) * by1] = column(pick1, line)

    all_directions(copy_coef, -1, lambda c: c.wait_recv())
    level0 = Level(x0, y0, depth, 1, *fw)
    level0.setup(lambda x: fine[1, x + 1], lambda x: f_top[x], HALO - reach, HALO + bx + reach)

    def coef1(x):
        coef = fine[1, 2 * x + 1] + fine[1, 2 * x + 2]
        m_coef[x + 1] = pair_rows(pair_lanes(coef, 1, add), pool_b, x, add) * 0.125

    planes(half - 3, half + bx1 + 3, coef1)
    level1 = Level(x1, y1, depth, 2, *mw)
    level1.setup(lambda x: m_coef[x + 1], lambda x: o_top[x + ring - half, by1 - half:by1 - half + y1],
                 half - 2, half + bx1 + 2)

    all_directions(copy_source, -1, lambda c: c.wait_recv())

    def load0(x):
        f_load[x] = level0.act[x] * fine[0, x + 1]

    planes(HALO - reach, HALO + bx + reach, load0)
    level0.smooth_fresh(f_load, f_u, f_smooth, HALO - reach, HALO + bx + reach)

    def restrict0(x):
        a, b = 2 * x, 2 * x + 1
        rest = (f_load[a] - level0.apply(f_smooth, a)) + (f_load[b] - level0.apply(f_smooth, b))
        m_load[x] = pair_rows(pair_lanes(rest, 1, add), pool_a, x, add)

    planes(half - 2, half + bx1 + 2, restrict0)

    even = lax.broadcasted_iota(jnp.int32, (by1, depth), 1) % 2 == 0
    for r in range(bx1 + 2):
        x = half - 1 + r
        packed[r] = jnp.where(even, m_load[x, half:half + by1], m_coef[x + 1, half:half + by1])
    all_directions(copy_outer, 1, lambda c: c.start())
    for r in range(bx1):
        outer[ring + r, by1:2 * by1] = packed[r + 1]

    level1.smooth_fresh(m_load, m_u, m_smooth, half - 2, half + bx1 + 2)
    for x in range(bx2):
        a, b = half + 2 * x, half + 2 * x + 1
        rest = (m_load[a] - level1.apply(m_smooth, a)) + (m_load[b] - level1.apply(m_smooth, b))
        load = pair_rows(pair_lanes(rest, 2, add), pool_d, x, add)
        mine[x:x + 1] = fold(load[quarter:quarter + by2])

    coarse_start()
    gathered[me] = mine[...]

    consts_arrived()
    lanes2 = lax.broadcasted_iota(jnp.int32, (ny2, depth), 1)
    chosen2 = lanes2 % 4 == lax.broadcasted_iota(jnp.int32, (ny2, depth), 0) % 4

    def unfold(places, x, row):
        for k in range(grp):
            line = places[(x // bx2) * grp + k, pl.ds(row, 1)]
            g_a[x, k * by2:(k + 1) * by2] = jnp.broadcast_to(line, (by2, depth))
        return jnp.where(chosen2, g_a[x], 0.0)

    def widen(values):
        return pair_lanes(pair_lanes(values, 1, add), 2, add)

    def unpack_consts(x):
        g_coef[x + 1] = widen(unfold(gathered_c, x, x % bx2))
        part = unfold(gathered_c, x, bx2)
        spot = lanes2 // (depth // bx2) == x % bx2
        top = jnp.max(jnp.where(spot, part, 0.0), axis=1, keepdims=True)
        g_top[x] = jnp.broadcast_to(top, (ny2, depth))

    planes(0, nx2, unpack_consts)
    level2 = Level(nx2, ny2, depth, 4, *gw)
    level2.setup(lambda x: g_coef[x + 1], lambda x: g_top[x], 0, nx2)

    all_directions(copy_outer, -1, lambda c: c.wait_recv())

    def unpack1(x):
        both = outer[x]
        o_load[x] = keep_lane(both, 0, 2)
        o_coef[x + 1] = keep_lane(both, 1, 2)

    planes(0, xo, unpack1)
    level_o = Level(xo, yo, depth, 2, *ow)
    level_o.setup(lambda x: o_coef[x + 1], lambda x: o_top[x], 1, xo - 1)
    level_o.smooth_fresh(o_load, o_u, o_smooth, 1, xo - 1)

    coarse_arrived()

    def unpack2(x):
        load = widen(unfold(gathered, x, x % bx2))
        g_r[x] = load
        g_d[x + 1] = load

    planes(0, nx2, unpack2)
    zero = jnp.zeros((ny2, depth), jnp.float32)

    def total(values):
        return jnp.sum(values, axis=(0, 1), keepdims=True)

    current = total(planes(0, nx2, lambda x, acc: acc + g_r[x] * g_r[x], zero))
    sol = spread[1]

    def first_sol(x):
        sol[x] = zero

    planes(0, nx2, first_sol)

    def iterate(_, current):
        def image(x, acc):
            applied = level2.apply(g_d, x)
            g_a[x] = applied
            return acc + g_d[x + 1] * applied

        step = current / total(planes(0, nx2, image, zero))

        def move(x, acc):
            sol[x] = sol[x] + step * g_d[x + 1]
            residual = g_r[x] - step * g_a[x]
            g_r[x] = residual
            return acc + residual * residual

        following = total(planes(0, nx2, move, zero))
        ratio = following / current

        def turn(x):
            g_d[x + 1] = g_r[x] + ratio * g_d[x + 1]

        planes(0, nx2, turn)
        return following

    lax.fori_loop(0, ITERS, iterate, current)

    pad = 3

    def cut(x):
        for k in range(grp):
            g_x[x + pad, k + 1] = sol[x, k * by2:(k + 1) * by2]

    planes(0, nx2, cut)

    wide_rows = spread[0]
    for x in range(2, xo - 2):
        parent = (x - ring) // 2
        for k in range(3):
            piece = g_x[w * bx2 + parent + pad, g + k]
            wide_rows[x, pl.ds(k * by1, by2, stride=2)] = piece
            wide_rows[x, pl.ds(k * by1 + 1, by2, stride=2)] = piece
        o_corr[x + 1] = o_smooth[x + 1] + level_o.act[x] * wide_rows[x]

    def put_outer(x, value):
        o_load[x] = value

    level_o.smooth_again(o_corr, o_load, o_e, o_u, ring - 1, ring + bx1 + 1, put_outer)

    fine_rows = spread[2]
    for x in range(HALO - 2, HALO + bx + 2):
        parent = o_load[(x - HALO) // 2 + ring, by1 - half:2 * by1 + half]
        fine_rows[x, pl.ds(0, y1, stride=2)] = parent
        fine_rows[x, pl.ds(1, y1, stride=2)] = parent
        f_smooth[x + 1] = f_smooth[x + 1] + level0.act[x] * fine_rows[x]

    def put_fine(x, value):
        out[x - HALO] = value[HALO:HALO + by]

    level0.smooth_again(f_smooth, f_load, f_e, f_u, HALO, HALO + bx, put_fine)

    for make in (copy_coef, copy_tops, copy_source, copy_outer):
        all_directions(make, 1, lambda c: c.wait_send())
    consts_sent()
    coarse_sent()


def shards(source, conductivity, ice_cells):
    wide, grp = lax.axis_size("wide"), lax.axis_size("grp")
    bx, by, depth = source.shape
    bx1, by1, bx2, by2 = bx // 2, by // 2, bx // 4, by // 4
    x0, y0 = bx + 2 * HALO, by + 2 * HALO
    x1, y1 = x0 // 2, y0 // 2
    ring = bx1 + 1
    xo, yo = bx1 + 2 * ring, 3 * by1
    nx2, ny2 = wide * bx2, grp * by2
    peers = wide * grp

    def block(*shape):
        return pltpu.VMEM(shape + (depth,), jnp.float32)

    def held(count, width):
        return [block(count + 1, width)] + [block(count, width) for _ in range(7)]

    dma = pltpu.SemaphoreType.DMA
    scratch = [
        block(2, x0 + 2, y0), held(x0, y0), block(x0, y0), block(x0 + 2, y0), block(x0 + 2, y0),
        block(x0, y0), block(x0, y0), block(x1, y0), block(x1, y0),
        block(x1, y1), block(x1 + 2, y1), held(x1, y1), block(x1 + 2, y1),
        block(x1 + 2, y1), block(bx1 + 2, by1),
        block(xo, yo), block(xo, yo), block(xo + 2, yo), block(xo, yo), held(xo, yo),
        block(xo + 2, yo), block(xo + 2, yo), block(xo, yo), block(xo + 2, yo),
        block(bx2, y1), block(bx1, by), block(bx2, by1), block(bx2), block(bx2 + 1),
        block(peers, bx2), block(peers, bx2 + 1),
        block(nx2 + 2, ny2), block(nx2, ny2), held(nx2, ny2),
        block(nx2 + 6, grp + 2, by2), block(nx2, ny2), block(nx2 + 2, ny2), block(nx2, ny2),
        [block(xo, yo), block(nx2, ny2), block(x0, y0)],
        block(9, bx), pltpu.VMEM((bx, by), jnp.int32), dma((3,)),
        *[dma((8,)) for _ in range(8)], *[dma((peers,)) for _ in range(4)],
    ]
    leaves, tree = jax.tree.flatten(scratch)

    def body(source_ref, conductivity_ref, ice_ref, out_ref, *refs):
        kernel(wide, grp, source_ref, conductivity_ref, ice_ref, out_ref,
               *jax.tree.unflatten(tree, refs))

    vmem = pl.BlockSpec(memory_space=pltpu.VMEM)
    return pl.pallas_call(
        body,
        out_shape=jax.ShapeDtypeStruct(source.shape, source.dtype),
        in_specs=[pl.BlockSpec(memory_space=pltpu.HBM)] * 3,
        out_specs=vmem,
        scratch_shapes=leaves,
        compiler_params=pltpu.CompilerParams(
            collective_id=0, has_side_effects=True, vmem_limit_bytes=48 * 1024 * 1024
        ),
    )(source, conductivity, ice_cells)


def solution(mesh):
    placed = (P("wide", "grp", None), P("wide", "grp", None), P("wide", "grp"))
    return jax.shard_map(
        shards, mesh=mesh, in_specs=placed, out_specs=P("wide", "grp", None), check_vma=False
    )
```

```python
import jax
import jax.numpy as jnp
from jax import lax
from jax.experimental import pallas as pl
from jax.experimental.pallas import tpu as pltpu
from jax.sharding import PartitionSpec as P

ITERS = 6
HALO = 8
TINY = 1e-30

cheb_center = (2.0 + 0.3) / 2.0
cheb_radius = (2.0 - 0.3) / 2.0
first_ratio = cheb_radius / cheb_center
second_ratio = 1.0 / (2.0 * cheb_center / cheb_radius - first_ratio)
carry_weight = second_ratio * first_ratio
fresh_weight = 2.0 * second_ratio / cheb_radius

DIRECTIONS = [(dx, dy) for dx in (-1, 0, 1) for dy in (-1, 0, 1) if (dx, dy) != (0, 0)]


def planes(low, high, body, carry=None):
    count = high - low
    unroll = count if count <= 32 else 4
    if carry is None:

        def step(x, _):
            body(x)
            return 0

        lax.fori_loop(low, high, step, 0, unroll=unroll)
        return None
    return lax.fori_loop(low, high, body, carry, unroll=unroll)


class Level:
    def __init__(self, count, width, depth, rep, wx, yp, ym, zp, zm, diag, inv, act):
        self.count, self.width, self.depth, self.rep = count, width, depth, rep
        self.wx, self.yp, self.ym, self.zp, self.zm = wx, yp, ym, zp, zm
        self.diag, self.inv, self.act = diag, inv, act

    def setup(self, coef, top, low, high):
        factor = float(self.rep)
        width, depth, rep = self.width, self.depth, self.rep
        lane = lax.broadcasted_iota(jnp.int32, (width, depth), 1)
        row = lax.broadcasted_iota(jnp.int32, (width, depth), 0)
        last_lane = lane >= depth - rep
        last_row = row == width - 1
        layer = ((lane // rep) * rep).astype(jnp.float32)

        def face(c, n):
            return factor * 2.0 * c * n / (c + n + TINY)

        self.wx[low] = face(coef(low), coef(low - 1))

        def body(x):
            c = coef(x)
            plus_x = face(c, coef(x + 1))
            self.wx[x + 1] = plus_x
            plus_y = face(c, jnp.where(last_row, 0.0, pltpu.roll(c, width - 1, 0)))
            plus_z = face(c, jnp.where(last_lane, 0.0, pltpu.roll(c, depth - rep, 1)))
            minus_y = pltpu.roll(plus_y, 1, 0)
            minus_z = pltpu.roll(plus_z, rep, 1)
            above = jnp.where(last_lane, factor * c, plus_z)
            diag = plus_x + self.wx[x] + plus_y + minus_y + above + minus_z
            self.yp[x] = plus_y
            self.ym[x] = minus_y
            self.zp[x] = plus_z
            self.zm[x] = minus_z
            self.diag[x] = diag
            self.inv[x] = 1.0 / jnp.maximum(diag, TINY)
            self.act[x] = (layer < top(x)).astype(jnp.float32)

        planes(low, high, body)

    def apply(self, v, x):
        here = v[x + 1]
        coupled = self.wx[x + 1] * v[x + 2] + self.wx[x] * v[x]
        coupled = coupled + self.yp[x] * pltpu.roll(here, self.width - 1, 0)
        coupled = coupled + self.ym[x] * pltpu.roll(here, 1, 0)
        coupled = coupled + self.zp[x] * pltpu.roll(here, self.depth - self.rep, 1)
        coupled = coupled + self.zm[x] * pltpu.roll(here, self.rep, 1)
        return self.act[x] * (self.diag[x] * here - coupled)

    def smooth_fresh(self, f, u, out, low, high):
        def first(x):
            u[x + 1] = f[x] * self.inv[x] * (1.0 / cheb_center)

        planes(low, high, first)
        low, high = (low + 1, high - 1) if low else (low, high)

        def second(x):
            residual = f[x] - self.apply(u, x)
            before = u[x + 1]
            update = carry_weight * before + fresh_weight * (residual * self.inv[x])
            out[x + 1] = before + update

        planes(low, high, second)

    def smooth_again(self, guess, f, e, u, low, high, put):
        def first(x):
            residual = f[x] - self.apply(guess, x)
            update = residual * self.inv[x] * (1.0 / cheb_center)
            e[x] = update
            u[x + 1] = guess[x + 1] + update

        planes(low - 1, high + 1, first)

        def second(x):
            residual = f[x] - self.apply(u, x)
            update = carry_weight * e[x] + fresh_weight * (residual * self.inv[x])
            put(x, u[x + 1] + update)

        planes(low, high, second)


class Coarse:
    def __init__(self, count, width, depth, px, mx, yp, ym, zp, zm, diag, act):
        self.count, self.width, self.depth = count, width, depth
        self.px, self.mx, self.yp, self.ym, self.zp, self.zm = px, mx, yp, ym, zp, zm
        self.diag, self.act = diag, act
        self.lane = lax.broadcasted_iota(jnp.int32, (width, depth), 1)
        self.slot = self.lane % 4

    def beside_x(self, v, x):
        here, depth = v[x + 1], self.depth
        after = jnp.where(self.slot < 3, pltpu.roll(here, depth - 1, 1), pltpu.roll(v[x + 2], 3, 1))
        before = jnp.where(self.slot > 0, pltpu.roll(here, 1, 1), pltpu.roll(v[x], depth - 3, 1))
        return here, after, before

    def setup(self, coef, top):
        width, depth = self.width, self.depth
        last_row = lax.broadcasted_iota(jnp.int32, (width, depth), 0) == width - 1
        last_lane = self.lane >= depth - 4
        layer = (self.lane - self.slot).astype(jnp.float32)

        def face(c, n):
            return 8.0 * c * n / (c + n + TINY)

        def body(x):
            c, after, before = self.beside_x(coef, x)
            plus_x, minus_x = face(c, after), face(c, before)
            plus_y = face(c, jnp.where(last_row, 0.0, pltpu.roll(c, width - 1, 0)))
            plus_z = face(c, jnp.where(last_lane, 0.0, pltpu.roll(c, depth - 4, 1)))
            minus_y = pltpu.roll(plus_y, 1, 0)
            minus_z = pltpu.roll(plus_z, 4, 1)
            above = jnp.where(last_lane, 4.0 * c, plus_z)
            self.diag[x] = plus_x + minus_x + plus_y + minus_y + above + minus_z
            self.px[x], self.mx[x] = plus_x, minus_x
            self.yp[x], self.ym[x] = plus_y, minus_y
            self.zp[x], self.zm[x] = plus_z, minus_z
            self.act[x] = (layer < top[x]).astype(jnp.float32)

        planes(0, self.count, body)

    def apply(self, v, x):
        here, after, before = self.beside_x(v, x)
        coupled = self.px[x] * after + self.mx[x] * before
        coupled = coupled + self.yp[x] * pltpu.roll(here, self.width - 1, 0)
        coupled = coupled + self.ym[x] * pltpu.roll(here, 1, 0)
        coupled = coupled + self.zp[x] * pltpu.roll(here, self.depth - 4, 1)
        coupled = coupled + self.zm[x] * pltpu.roll(here, 4, 1)
        return here, self.act[x] * (self.diag[x] * here - coupled)


def pair_lanes(values, rep, join):
    width, depth = values.shape
    lane = lax.broadcasted_iota(jnp.int32, (width, depth), 1)
    lower = (lane // rep) % 2 == 0
    partner = jnp.where(lower, pltpu.roll(values, depth - rep, 1), pltpu.roll(values, rep, 1))
    return join(values, partner)


def pair_rows(values, buffer, x, join):
    half = values.shape[0] // 2
    buffer[x] = values
    return join(buffer[x, pl.ds(0, half, stride=2)], buffer[x, pl.ds(1, half, stride=2)])


def keep_lane(values, slot, slots):
    width, depth = values.shape
    lane = lax.broadcasted_iota(jnp.int32, (width, depth), 1)
    kept = jnp.where(lane % slots == slot, values, 0.0)
    if slot:
        kept = pltpu.roll(kept, depth - slot, 1)
    shift = 1
    while shift < slots:
        kept = kept + pltpu.roll(kept, shift, 1)
        shift *= 2
    return kept


def add(a, b):
    return a + b


def selector(count, first, stride, depth):
    rows = lax.broadcasted_iota(jnp.int32, (count, depth), 0)
    lanes = lax.broadcasted_iota(jnp.int32, (count, depth), 1)
    return (lanes == rows * stride + first).astype(jnp.float32)


def column(pick, row):
    return jnp.broadcast_to(jnp.sum(pick * row, axis=1, keepdims=True), pick.shape)


def kernel(wide, grp, source, conductivity, ice, out, *scratch):
    (fine, fw, f_load, f_u, f_smooth, f_e, f_top, pool_a, pool_b,
     m_load, m_coef, mw, m_u, m_smooth, packed,
     outer, o_load, o_coef, o_top, ow, o_u, o_smooth, o_e, o_corr,
     pool_d, pool_g, pool_h, mine, mine_c, gathered, gathered_c,
     g_coef, g_top, gw, g_x, g_r, g_p, g_s, g_a, sol,
     wide_rows, fine_rows, tops, ice_here, sem_in,
     send_a, recv_a, send_t, recv_t, send_s, recv_s, send_b, recv_b,
     send_c, recv_c, send_g, recv_g) = scratch
    bx, by, depth = source.shape
    bx1, by1, bx2, by2 = bx // 2, by // 2, bx // 4, by // 4
    x0, y0 = bx + 2 * HALO, by + 2 * HALO
    x1, y1 = x0 // 2, y0 // 2
    ring = bx1 + 1
    xo, yo = bx1 + 2 * ring, 3 * by1
    nx2, ny2 = wide * bx2, grp * by2
    half, quarter = HALO // 2, HALO // 4
    w, g = lax.axis_index("wide"), lax.axis_index("grp")
    peers = wide * grp
    me = w * grp + g

    middle = (pl.ds(HALO + 1, bx), pl.ds(HALO, by))
    load_source = pltpu.make_async_copy(source, fine.at[(0,) + middle], sem_in.at[0])
    load_coef = pltpu.make_async_copy(conductivity, fine.at[(1,) + middle], sem_in.at[1])
    load_ice = pltpu.make_async_copy(ice, ice_here, sem_in.at[2])
    load_ice.start()
    load_coef.start()
    load_source.start()

    for channel in range(2):
        for x in range(x0 + 2):
            if HALO < x <= HALO + bx:
                fine[channel, x, 0:HALO] = jnp.zeros((HALO, depth), jnp.float32)
                fine[channel, x, HALO + by:y0] = jnp.zeros((HALO, depth), jnp.float32)
            else:
                fine[channel, x] = jnp.zeros((y0, depth), jnp.float32)

    def clear(ref):
        def body(x):
            ref[x] = jnp.zeros(ref.shape[1:], ref.dtype)

        planes(0, ref.shape[0], body)

    clear(outer)
    clear(tops)

    barrier = pltpu.get_barrier_semaphore()

    def mesh_id(other):
        return (other // grp, lax.rem(other, grp))

    def greet(d, _):
        pl.semaphore_signal(barrier, inc=1, device_id=mesh_id(lax.rem(me + d, peers)),
                            device_id_type=pl.DeviceIdType.MESH)
        return 0

    lax.fori_loop(1, peers, greet, 0)

    for ref in (f_u, f_smooth, m_u, m_smooth, o_u, o_smooth, o_corr, g_r, sol, m_coef, o_coef, g_coef):
        ref[0] = jnp.zeros(ref.shape[1:], jnp.float32)
        ref[ref.shape[0] - 1] = jnp.zeros(ref.shape[1:], jnp.float32)
    clear(g_x)

    load_ice.wait()
    tops[4, :, 0:by] = ice_here[...].astype(jnp.float32)
    load_coef.wait()
    slot = lax.broadcasted_iota(jnp.int32, (by2, depth), 1) % 4
    pick2 = selector(by2, 0, 4, depth)
    first_slot = lax.rem(w * bx2, 4)
    consts = jnp.zeros((by2, depth), jnp.float32)
    for x in range(bx2):
        coef = None
        for r in range(2):
            a = HALO + 1 + 4 * x + 2 * r
            pair = fine[1, a, HALO:HALO + by] + fine[1, a + 1, HALO:HALO + by]
            pair = pair_rows(pair_lanes(pair, 1, add), pool_g, 2 * x + r, add) * 0.125
            coef = pair if coef is None else coef + pair
        coef = pair_rows(pair_lanes(coef, 2, add), pool_h, x, add) * 0.125
        top = jnp.max(tops[4, 4 * x:4 * x + 4], axis=0, keepdims=True)
        top = jnp.maximum(top, pltpu.roll(top, depth - 1, 1))
        top = jnp.maximum(top, pltpu.roll(top, depth - 2, 1))
        here = first_slot + x
        consts = jnp.where(slot == here, coef, consts)
        consts = jnp.where(slot == lax.rem(here + 2, 4), column(pick2, top), consts)
    mine_c[...] = consts

    load_source.wait()
    pl.semaphore_wait(barrier, peers - 1)

    def inside(dx, dy):
        return (w + dx >= 0) & (w + dx < wide) & (g + dy >= 0) & (g + dy < grp)

    def remote(src, dst, send, recv, device):
        return pltpu.make_async_remote_copy(
            src_ref=src, dst_ref=dst, send_sem=send, recv_sem=recv,
            device_id=device, device_id_type=pl.DeviceIdType.MESH)

    def copy_fine(channel, send, recv):
        def make(k, dx, dy):
            rows = (HALO - 2 if dy == 0 else HALO - 3) + channel
            src_x, dst_x, len_x = {
                1: (1 + HALO + bx - rows, 1 + HALO - rows, rows),
                0: (1 + HALO, 1 + HALO, bx),
                -1: (1 + HALO, 1 + HALO + bx, rows),
            }[dx]
            src_y, dst_y, len_y = {
                1: (by, 0, HALO), 0: (HALO, HALO, by), -1: (HALO, HALO + by, HALO)
            }[dy]
            return remote(
                fine.at[channel, pl.ds(src_x, len_x), pl.ds(src_y, len_y)],
                fine.at[channel, pl.ds(dst_x, len_x), pl.ds(dst_y, len_y)],
                send.at[k], recv.at[k], (w + dx, g + dy))

        return make

    copy_coef = copy_fine(1, send_a, recv_a)
    copy_source = copy_fine(0, send_s, recv_s)

    def copy_tops(k, dx, dy):
        return remote(tops.at[4], tops.at[(1 - dx) * 3 + 1 - dy],
                      send_t.at[k], recv_t.at[k], (w + dx, g + dy))

    def copy_outer(k, dx, dy):
        src_x, dst_x, len_x = {
            1: (0, 0, ring), 0: (1, ring, bx1), -1: (1, ring + bx1, ring)
        }[dx]
        dst_y = {1: 0, 0: by1, -1: 2 * by1}[dy]
        return remote(packed.at[pl.ds(src_x, len_x)],
                      outer.at[pl.ds(dst_x, len_x), pl.ds(dst_y, by1)],
                      send_b.at[k], recv_b.at[k], (w + dx, g + dy))

    def all_directions(make, sign, act):
        for k, (dx, dy) in enumerate(DIRECTIONS):
            @pl.when(inside(sign * dx, sign * dy))
            def _():
                act(make(k, dx, dy))

    def copy_all(block, places, send, recv):
        def make(d, owner, to):
            return remote(block, places.at[owner], send.at[d], recv.at[d], mesh_id(to))

        def start():
            def body(d, _):
                make(d, me, lax.rem(me + d, peers)).start()
                return 0
            lax.fori_loop(1, peers, body, 0)

        def arrived():
            def body(d, _):
                make(d, lax.rem(me + peers - d, peers), me).wait_recv()
                return 0
            lax.fori_loop(1, peers, body, 0)

        def sent():
            def body(d, _):
                make(d, me, lax.rem(me + d, peers)).wait_send()
                return 0
            lax.fori_loop(1, peers, body, 0)

        return start, arrived, sent

    coarse_start, coarse_arrived, coarse_sent = copy_all(mine, gathered, send_c, recv_c)
    consts_start, consts_arrived, consts_sent = copy_all(mine_c, gathered_c, send_g, recv_g)

    all_directions(copy_coef, 1, lambda c: c.start())
    all_directions(copy_tops, 1, lambda c: c.start())
    all_directions(copy_source, 1, lambda c: c.start())
    consts_start()
    gathered_c[me] = mine_c[...]

    all_directions(copy_tops, -1, lambda c: c.wait_recv())
    reach = HALO - 2
    picks = (selector(HALO, by - HALO, 1, depth), selector(by, 0, 1, depth),
             selector(HALO, 0, 1, depth))
    starts = (0, HALO, HALO + by)
    for x in range(HALO - reach, HALO + bx + reach):
        row = x - HALO + bx
        for k in range(3):
            line = tops[row // bx * 3 + k, row % bx:row % bx + 1]
            f_top[x, starts[k]:starts[k] + picks[k].shape[0]] = column(picks[k], line)
    pick1 = selector(by1, 0, 2, depth)
    for x in range(1, xo - 1):
        row = 2 * (x - 1)
        for k in range(3):
            line = jnp.max(tops[row // bx * 3 + k, row % bx:row % bx + 2], axis=0, keepdims=True)
            line = jnp.maximum(line, pltpu.roll(line, depth - 1, 1))
            o_top[x, k * by1:(k + 1) * by1] = column(pick1, line)

    all_directions(copy_coef, -1, lambda c: c.wait_recv())
    level0 = Level(x0, y0, depth, 1, *fw)
    level0.setup(lambda x: fine[1, x + 1], lambda x: f_top[x], HALO - reach, HALO + bx + reach)

    def coef1(x):
        coef = fine[1, 2 * x + 1] + fine[1, 2 * x + 2]
        m_coef[x + 1] = pair_rows(pair_lanes(coef, 1, add), pool_b, x, add) * 0.125

    planes(half - 3, half + bx1 + 3, coef1)
    level1 = Level(x1, y1, depth, 2, *mw)
    level1.setup(lambda x: m_coef[x + 1], lambda x: o_top[x + ring - half, by1 - half:by1 - half + y1],
                 half - 2, half + bx1 + 2)

    all_directions(copy_source, -1, lambda c: c.wait_recv())

    def load0(x):
        f_load[x] = level0.act[x] * fine[0, x + 1]

    planes(HALO - reach, HALO + bx + reach, load0)
    level0.smooth_fresh(f_load, f_u, f_smooth, HALO - reach, HALO + bx + reach)

    def restrict0(x):
        a, b = 2 * x, 2 * x + 1
        rest = (f_load[a] - level0.apply(f_smooth, a)) + (f_load[b] - level0.apply(f_smooth, b))
        m_load[x] = pair_rows(pair_lanes(rest, 1, add), pool_a, x, add)

    planes(half - 2, half + bx1 + 2, restrict0)

    even = lax.broadcasted_iota(jnp.int32, (by1, depth), 1) % 2 == 0
    for r in range(bx1 + 2):
        x = half - 1 + r
        packed[r] = jnp.where(even, m_load[x, half:half + by1], m_coef[x + 1, half:half + by1])
    all_directions(copy_outer, 1, lambda c: c.start())
    for r in range(bx1):
        outer[ring + r, by1:2 * by1] = packed[r + 1]

    level1.smooth_fresh(m_load, m_u, m_smooth, half - 2, half + bx1 + 2)
    rows = by2 // 2
    loads = jnp.zeros((rows, depth), jnp.float32)
    for x in range(bx2):
        a, b = half + 2 * x, half + 2 * x + 1
        rest = (m_load[a] - level1.apply(m_smooth, a)) + (m_load[b] - level1.apply(m_smooth, b))
        load = pair_rows(pair_lanes(rest, 2, add), pool_d, x, add)
        here = first_slot + x
        loads = jnp.where(slot[:rows] == here, load[quarter:quarter + rows], loads)
        loads = jnp.where(slot[:rows] == lax.rem(here + 2, 4),
                          load[quarter + rows:quarter + by2], loads)
    mine[...] = loads

    coarse_start()
    gathered[me] = mine[...]

    consts_arrived()

    def unpair(places, x, k):
        near, far = places[2 * x * grp + k], places[(2 * x + 1) * grp + k]
        lower = slot[:near.shape[0]] < 2
        return (jnp.where(lower, near, far),
                jnp.where(lower, pltpu.roll(near, depth - 2, 1), pltpu.roll(far, 2, 1)))

    def unpack_consts(x):
        for k in range(grp):
            own = pl.ds(k * by2, by2)
            g_coef[x + 1, own], g_top[x, own] = unpair(gathered_c, x, k)

    nq = nx2 // 4
    planes(0, nq, unpack_consts)
    level2 = Coarse(nq, ny2, depth, *gw)
    level2.setup(g_coef, g_top)
    zero = jnp.zeros((ny2, depth), jnp.float32)

    def reset(x):
        g_p[x] = zero
        g_s[x] = zero
        sol[x + 1] = zero

    planes(0, nq, reset)

    all_directions(copy_outer, -1, lambda c: c.wait_recv())

    def unpack1(x):
        both = outer[x]
        o_load[x] = keep_lane(both, 0, 2)
        o_coef[x + 1] = keep_lane(both, 1, 2)

    planes(0, xo, unpack1)
    level_o = Level(xo, yo, depth, 2, *ow)
    level_o.setup(lambda x: o_coef[x + 1], lambda x: o_top[x], 1, xo - 1)
    level_o.smooth_fresh(o_load, o_u, o_smooth, 1, xo - 1)

    coarse_arrived()

    def unpack_loads(x):
        for k in range(grp):
            low, high = unpair(gathered, x, k)
            g_r[x + 1, k * by2:k * by2 + rows] = low
            g_r[x + 1, k * by2 + rows:(k + 1) * by2] = high

    planes(0, nq, unpack_loads)

    def total(values):
        return jnp.sum(values, axis=(0, 1), keepdims=True)

    def iterate(_, carry):
        before, step_before = carry

        def image(x, sums):
            here, applied = level2.apply(g_r, x)
            g_a[x] = applied
            return sums[0] + here * here, sums[1] + here * applied

        squares, products = planes(0, nq, image, (zero, zero))
        current, curvature = total(squares), total(products)
        ratio = current / before
        step = current / (curvature - ratio * current / step_before)

        def move(x):
            direction = g_r[x + 1] + ratio * g_p[x]
            applied = g_a[x] + ratio * g_s[x]
            g_p[x], g_s[x] = direction, applied
            sol[x + 1] = sol[x + 1] + step * direction
            g_r[x + 1] = g_r[x + 1] - step * applied

        planes(0, nq, move)
        return current, step

    one = jnp.ones((1, 1), jnp.float32)
    lax.fori_loop(0, ITERS, iterate, (one * jnp.inf, one))

    spans = range((2 - ring) // 2, (xo - 3 - ring) // 2 + 1)
    slot2 = level2.slot
    for p in spans:
        x = w * bx2 + p + 4
        kept = jnp.where(slot2 == lax.rem(x, 4), sol[x // 4], 0.0)
        kept = pair_lanes(pair_lanes(kept, 1, add), 2, add)
        for k in range(grp):
            g_x[p - spans[0], k + 1] = kept[k * by2:(k + 1) * by2]

    for x in range(2, xo - 2):
        parent = (x - ring) // 2
        for k in range(3):
            piece = g_x[parent - spans[0], g + k]
            wide_rows[x, pl.ds(k * by1, by2, stride=2)] = piece
            wide_rows[x, pl.ds(k * by1 + 1, by2, stride=2)] = piece
        o_corr[x + 1] = o_smooth[x + 1] + level_o.act[x] * wide_rows[x]

    def put_outer(x, value):
        o_load[x] = value

    level_o.smooth_again(o_corr, o_load, o_e, o_u, ring - 1, ring + bx1 + 1, put_outer)

    for x in range(HALO - 2, HALO + bx + 2):
        parent = o_load[(x - HALO) // 2 + ring, by1 - half:2 * by1 + half]
        fine_rows[x, pl.ds(0, y1, stride=2)] = parent
        fine_rows[x, pl.ds(1, y1, stride=2)] = parent
        f_smooth[x + 1] = f_smooth[x + 1] + level0.act[x] * fine_rows[x]

    def put_fine(x, value):
        out[x - HALO] = value[HALO:HALO + by]

    level0.smooth_again(f_smooth, f_load, f_e, f_u, HALO, HALO + bx, put_fine)

    for make in (copy_coef, copy_tops, copy_source, copy_outer):
        all_directions(make, 1, lambda c: c.wait_send())
    consts_sent()
    coarse_sent()


def shards(source, conductivity, ice_cells):
    wide, grp = lax.axis_size("wide"), lax.axis_size("grp")
    bx, by, depth = source.shape
    bx1, by1, bx2, by2 = bx // 2, by // 2, bx // 4, by // 4
    x0, y0 = bx + 2 * HALO, by + 2 * HALO
    x1, y1 = x0 // 2, y0 // 2
    ring = bx1 + 1
    xo, yo = bx1 + 2 * ring, 3 * by1
    nq, ny2 = wide * bx2 // 4, grp * by2
    peers = wide * grp

    def block(*shape):
        return pltpu.VMEM(shape + (depth,), jnp.float32)

    def held(count, width):
        return [block(count + 1, width)] + [block(count, width) for _ in range(7)]

    dma = pltpu.SemaphoreType.DMA
    scratch = [
        block(2, x0 + 2, y0), held(x0, y0), block(x0, y0), block(x0 + 2, y0), block(x0 + 2, y0),
        block(x0, y0), block(x0, y0), block(x1, y0), block(x1, y0),
        block(x1, y1), block(x1 + 2, y1), held(x1, y1), block(x1 + 2, y1),
        block(x1 + 2, y1), block(bx1 + 2, by1),
        block(xo, yo), block(xo, yo), block(xo + 2, yo), block(xo, yo), held(xo, yo),
        block(xo + 2, yo), block(xo + 2, yo), block(xo, yo), block(xo + 2, yo),
        block(bx2, y1), block(bx1, by), block(bx2, by1), block(by2 // 2), block(by2),
        block(peers, by2 // 2), block(peers, by2),
        block(nq + 2, ny2), block(nq, ny2), [block(nq, ny2) for _ in range(8)],
        block(xo // 2, grp + 2, by2), block(nq + 2, ny2), block(nq, ny2), block(nq, ny2),
        block(nq, ny2), block(nq + 2, ny2),
        block(xo, yo), block(x0, y0),
        block(9, bx), pltpu.VMEM((bx, by), jnp.int32), dma((3,)),
        *[dma((8,)) for _ in range(8)], *[dma((peers,)) for _ in range(4)],
    ]
    leaves, tree = jax.tree.flatten(scratch)

    def body(source_ref, conductivity_ref, ice_ref, out_ref, *refs):
        kernel(wide, grp, source_ref, conductivity_ref, ice_ref, out_ref,
               *jax.tree.unflatten(tree, refs))

    vmem = pl.BlockSpec(memory_space=pltpu.VMEM)
    return pl.pallas_call(
        body,
        out_shape=jax.ShapeDtypeStruct(source.shape, source.dtype),
        in_specs=[pl.BlockSpec(memory_space=pltpu.HBM)] * 3,
        out_specs=vmem,
        scratch_shapes=leaves,
        compiler_params=pltpu.CompilerParams(
            collective_id=0, has_side_effects=True, vmem_limit_bytes=64 * 1024 * 1024
        ),
    )(source, conductivity, ice_cells)


def solution(mesh):
    placed = (P("wide", "grp", None), P("wide", "grp", None), P("wide", "grp"))
    return jax.shard_map(
        shards, mesh=mesh, in_specs=placed, out_specs=P("wide", "grp", None), check_vma=False
    )
```

```python
import jax
import jax.numpy as jnp
from jax import lax
from jax.experimental import pallas as pl
from jax.experimental.pallas import tpu as pltpu
from jax.sharding import PartitionSpec as P

ITERS = 6
HALO = 8
TINY = 1e-30

cheb_center = (2.0 + 0.3) / 2.0
cheb_radius = (2.0 - 0.3) / 2.0
first_ratio = cheb_radius / cheb_center
second_ratio = 1.0 / (2.0 * cheb_center / cheb_radius - first_ratio)
carry_weight = second_ratio * first_ratio
fresh_weight = 2.0 * second_ratio / cheb_radius

DIRECTIONS = [(dx, dy) for dx in (-1, 0, 1) for dy in (-1, 0, 1) if (dx, dy) != (0, 0)]


def planes(low, high, body, carry=None):
    count = high - low
    unroll = count if count <= 32 else 4
    if carry is None:

        def step(x, _):
            body(x)
            return 0

        lax.fori_loop(low, high, step, 0, unroll=unroll)
        return None
    return lax.fori_loop(low, high, body, carry, unroll=unroll)


class Level:
    def __init__(self, count, width, depth, rep, wx, yp, ym, zp, zm, diag, inv, act):
        self.count, self.width, self.depth, self.rep = count, width, depth, rep
        self.wx, self.yp, self.ym, self.zp, self.zm = wx, yp, ym, zp, zm
        self.diag, self.inv, self.act = diag, inv, act

    def setup(self, coef, top, low, high):
        factor = float(self.rep)
        width, depth, rep = self.width, self.depth, self.rep
        lane = lax.broadcasted_iota(jnp.int32, (width, depth), 1)
        row = lax.broadcasted_iota(jnp.int32, (width, depth), 0)
        last_lane = lane >= depth - rep
        last_row = row == width - 1
        layer = ((lane // rep) * rep).astype(jnp.float32)

        def face(c, n):
            return factor * 2.0 * c * n / (c + n + TINY)

        self.wx[low] = face(coef(low), coef(low - 1))

        def body(x):
            c = coef(x)
            plus_x = face(c, coef(x + 1))
            self.wx[x + 1] = plus_x
            plus_y = face(c, jnp.where(last_row, 0.0, pltpu.roll(c, width - 1, 0)))
            plus_z = face(c, jnp.where(last_lane, 0.0, pltpu.roll(c, depth - rep, 1)))
            minus_y = pltpu.roll(plus_y, 1, 0)
            minus_z = pltpu.roll(plus_z, rep, 1)
            above = jnp.where(last_lane, factor * c, plus_z)
            diag = plus_x + self.wx[x] + plus_y + minus_y + above + minus_z
            self.yp[x] = plus_y
            self.ym[x] = minus_y
            self.zp[x] = plus_z
            self.zm[x] = minus_z
            self.diag[x] = diag
            self.inv[x] = 1.0 / jnp.maximum(diag, TINY)
            self.act[x] = (layer < top(x)).astype(jnp.float32)

        planes(low, high, body)

    def apply(self, v, x):
        here = v[x + 1]
        coupled = self.wx[x + 1] * v[x + 2] + self.wx[x] * v[x]
        coupled = coupled + self.yp[x] * pltpu.roll(here, self.width - 1, 0)
        coupled = coupled + self.ym[x] * pltpu.roll(here, 1, 0)
        coupled = coupled + self.zp[x] * pltpu.roll(here, self.depth - self.rep, 1)
        coupled = coupled + self.zm[x] * pltpu.roll(here, self.rep, 1)
        return self.act[x] * (self.diag[x] * here - coupled)

    def smooth_fresh(self, f, u, out, low, high):
        def first(x):
            u[x + 1] = f[x] * self.inv[x] * (1.0 / cheb_center)

        planes(low, high, first)
        low, high = (low + 1, high - 1) if low else (low, high)

        def second(x):
            residual = f[x] - self.apply(u, x)
            before = u[x + 1]
            update = carry_weight * before + fresh_weight * (residual * self.inv[x])
            out[x + 1] = before + update

        planes(low, high, second)

    def smooth_again(self, guess, f, e, u, low, high, put):
        def first(x):
            residual = f[x] - self.apply(guess, x)
            update = residual * self.inv[x] * (1.0 / cheb_center)
            e[x] = update
            u[x + 1] = guess[x + 1] + update

        planes(low - 1, high + 1, first)

        def second(x):
            residual = f[x] - self.apply(u, x)
            update = carry_weight * e[x] + fresh_weight * (residual * self.inv[x])
            put(x, u[x + 1] + update)

        planes(low, high, second)


class Coarse:
    def __init__(self, count, width, depth, px, mx, yp, ym, zp, zm, diag, act):
        self.count, self.width, self.depth = count, width, depth
        self.px, self.mx, self.yp, self.ym, self.zp, self.zm = px, mx, yp, ym, zp, zm
        self.diag, self.act = diag, act
        self.lane = lax.broadcasted_iota(jnp.int32, (width, depth), 1)
        self.slot = self.lane % 4

    def beside_x(self, v, x):
        here, depth = v[x + 1], self.depth
        after = jnp.where(self.slot < 3, pltpu.roll(here, depth - 1, 1), pltpu.roll(v[x + 2], 3, 1))
        before = jnp.where(self.slot > 0, pltpu.roll(here, 1, 1), pltpu.roll(v[x], depth - 3, 1))
        return here, after, before

    def setup(self, coef, top):
        width, depth = self.width, self.depth
        last_row = lax.broadcasted_iota(jnp.int32, (width, depth), 0) == width - 1
        last_lane = self.lane >= depth - 4
        layer = (self.lane - self.slot).astype(jnp.float32)

        def face(c, n):
            return 8.0 * c * n / (c + n + TINY)

        def body(x):
            c, after, before = self.beside_x(coef, x)
            plus_x, minus_x = face(c, after), face(c, before)
            plus_y = face(c, jnp.where(last_row, 0.0, pltpu.roll(c, width - 1, 0)))
            plus_z = face(c, jnp.where(last_lane, 0.0, pltpu.roll(c, depth - 4, 1)))
            minus_y = pltpu.roll(plus_y, 1, 0)
            minus_z = pltpu.roll(plus_z, 4, 1)
            above = jnp.where(last_lane, 4.0 * c, plus_z)
            self.diag[x] = plus_x + minus_x + plus_y + minus_y + above + minus_z
            self.px[x], self.mx[x] = plus_x, minus_x
            self.yp[x], self.ym[x] = plus_y, minus_y
            self.zp[x], self.zm[x] = plus_z, minus_z
            self.act[x] = (layer < top[x]).astype(jnp.float32)

        planes(0, self.count, body)

    def apply(self, v, x):
        here, after, before = self.beside_x(v, x)
        coupled = self.px[x] * after + self.mx[x] * before
        coupled = coupled + self.yp[x] * pltpu.roll(here, self.width - 1, 0)
        coupled = coupled + self.ym[x] * pltpu.roll(here, 1, 0)
        coupled = coupled + self.zp[x] * pltpu.roll(here, self.depth - 4, 1)
        coupled = coupled + self.zm[x] * pltpu.roll(here, 4, 1)
        return here, self.act[x] * (self.diag[x] * here - coupled)


def pair_lanes(values, rep, join):
    width, depth = values.shape
    lane = lax.broadcasted_iota(jnp.int32, (width, depth), 1)
    lower = (lane // rep) % 2 == 0
    partner = jnp.where(lower, pltpu.roll(values, depth - rep, 1), pltpu.roll(values, rep, 1))
    return join(values, partner)


def pair_rows(values, buffer, x, join):
    half = values.shape[0] // 2
    buffer[x] = values
    return join(buffer[x, pl.ds(0, half, stride=2)], buffer[x, pl.ds(1, half, stride=2)])


def keep_lane(values, slot, slots):
    width, depth = values.shape
    lane = lax.broadcasted_iota(jnp.int32, (width, depth), 1)
    kept = jnp.where(lane % slots == slot, values, 0.0)
    if slot:
        kept = pltpu.roll(kept, depth - slot, 1)
    shift = 1
    while shift < slots:
        kept = kept + pltpu.roll(kept, shift, 1)
        shift *= 2
    return kept


def add(a, b):
    return a + b


def selector(count, first, stride, depth):
    rows = lax.broadcasted_iota(jnp.int32, (count, depth), 0)
    lanes = lax.broadcasted_iota(jnp.int32, (count, depth), 1)
    return (lanes == rows * stride + first).astype(jnp.float32)


def column(pick, row):
    return jnp.broadcast_to(jnp.sum(pick * row, axis=1, keepdims=True), pick.shape)


def kernel(wide, grp, source, conductivity, ice, out, *scratch):
    (fine, fw, f_load, f_u, f_smooth, f_e, f_top, pool_a, pool_b,
     m_load, m_coef, mw, m_u, m_smooth, packed,
     outer, o_load, o_coef, o_top, ow, o_u, o_smooth, o_e, o_corr,
     pool_d, pool_g, pool_h, mine, mine_c, gathered, gathered_c,
     g_coef, g_top, gw, g_x, g_r, g_p, g_s, g_a, sol,
     wide_rows, fine_rows, tops, ice_here, result, sem_in, sem_out,
     send_a, recv_a, send_t, recv_t, send_s, recv_s, send_b, recv_b,
     send_c, recv_c, send_g, recv_g) = scratch
    bx, by, depth = source.shape
    bx1, by1, bx2, by2 = bx // 2, by // 2, bx // 4, by // 4
    x0, y0 = bx + 2 * HALO, by + 2 * HALO
    x1, y1 = x0 // 2, y0 // 2
    ring = bx1 + 1
    xo, yo = bx1 + 2 * ring, 3 * by1
    nx2, ny2 = wide * bx2, grp * by2
    half, quarter = HALO // 2, HALO // 4
    w, g = lax.axis_index("wide"), lax.axis_index("grp")
    peers = wide * grp
    me = w * grp + g

    middle = (pl.ds(HALO + 1, bx), pl.ds(HALO, by))
    load_source = pltpu.make_async_copy(source, fine.at[(0,) + middle], sem_in.at[0])
    load_coef = pltpu.make_async_copy(conductivity, fine.at[(1,) + middle], sem_in.at[1])
    load_ice = pltpu.make_async_copy(ice, ice_here, sem_in.at[2])
    load_ice.start()
    load_coef.start()
    load_source.start()

    for channel in range(2):
        for x in range(x0 + 2):
            if HALO < x <= HALO + bx:
                fine[channel, x, 0:HALO] = jnp.zeros((HALO, depth), jnp.float32)
                fine[channel, x, HALO + by:y0] = jnp.zeros((HALO, depth), jnp.float32)
            else:
                fine[channel, x] = jnp.zeros((y0, depth), jnp.float32)

    def clear(ref):
        def body(x):
            ref[x] = jnp.zeros(ref.shape[1:], ref.dtype)

        planes(0, ref.shape[0], body)

    clear(outer)
    clear(tops)

    barrier = pltpu.get_barrier_semaphore()

    def mesh_id(other):
        return (other // grp, lax.rem(other, grp))

    def greet(d, _):
        pl.semaphore_signal(barrier, inc=1, device_id=mesh_id(lax.rem(me + d, peers)),
                            device_id_type=pl.DeviceIdType.MESH)
        return 0

    lax.fori_loop(1, peers, greet, 0)

    for ref in (f_u, f_smooth, m_u, m_smooth, o_u, o_smooth, o_corr, g_r, sol, m_coef, o_coef, g_coef):
        ref[0] = jnp.zeros(ref.shape[1:], jnp.float32)
        ref[ref.shape[0] - 1] = jnp.zeros(ref.shape[1:], jnp.float32)
    clear(g_x)

    load_ice.wait()
    tops[4, :, 0:by] = ice_here[...].astype(jnp.float32)
    load_coef.wait()
    pl.semaphore_wait(barrier, peers - 1)

    def inside(dx, dy):
        return (w + dx >= 0) & (w + dx < wide) & (g + dy >= 0) & (g + dy < grp)

    def remote(src, dst, send, recv, device):
        return pltpu.make_async_remote_copy(
            src_ref=src, dst_ref=dst, send_sem=send, recv_sem=recv,
            device_id=device, device_id_type=pl.DeviceIdType.MESH)

    def copy_fine(channel, send, recv):
        def make(k, dx, dy):
            rows = (HALO - 2 if dy == 0 else HALO - 3) + channel
            src_x, dst_x, len_x = {
                1: (1 + HALO + bx - rows, 1 + HALO - rows, rows),
                0: (1 + HALO, 1 + HALO, bx),
                -1: (1 + HALO, 1 + HALO + bx, rows),
            }[dx]
            src_y, dst_y, len_y = {
                1: (by, 0, HALO), 0: (HALO, HALO, by), -1: (HALO, HALO + by, HALO)
            }[dy]
            return remote(
                fine.at[channel, pl.ds(src_x, len_x), pl.ds(src_y, len_y)],
                fine.at[channel, pl.ds(dst_x, len_x), pl.ds(dst_y, len_y)],
                send.at[k], recv.at[k], (w + dx, g + dy))

        return make

    copy_coef = copy_fine(1, send_a, recv_a)
    copy_source = copy_fine(0, send_s, recv_s)

    def copy_tops(k, dx, dy):
        return remote(tops.at[4], tops.at[(1 - dx) * 3 + 1 - dy],
                      send_t.at[k], recv_t.at[k], (w + dx, g + dy))

    def copy_outer(k, dx, dy):
        src_x, dst_x, len_x = {
            1: (0, 0, ring), 0: (1, ring, bx1), -1: (1, ring + bx1, ring)
        }[dx]
        dst_y = {1: 0, 0: by1, -1: 2 * by1}[dy]
        return remote(packed.at[pl.ds(src_x, len_x)],
                      outer.at[pl.ds(dst_x, len_x), pl.ds(dst_y, by1)],
                      send_b.at[k], recv_b.at[k], (w + dx, g + dy))

    def all_directions(make, sign, act):
        for k, (dx, dy) in enumerate(DIRECTIONS):
            @pl.when(inside(sign * dx, sign * dy))
            def _():
                act(make(k, dx, dy))

    def copy_all(block, places, send, recv):
        def make(d, owner, to):
            return remote(block, places.at[owner], send.at[d], recv.at[d], mesh_id(to))

        def start():
            def body(d, _):
                make(d, me, lax.rem(me + d, peers)).start()
                return 0
            lax.fori_loop(1, peers, body, 0)

        def arrived():
            def body(d, _):
                make(d, lax.rem(me + peers - d, peers), me).wait_recv()
                return 0
            lax.fori_loop(1, peers, body, 0)

        def sent():
            def body(d, _):
                make(d, me, lax.rem(me + d, peers)).wait_send()
                return 0
            lax.fori_loop(1, peers, body, 0)

        return start, arrived, sent

    coarse_start, coarse_arrived, coarse_sent = copy_all(mine, gathered, send_c, recv_c)
    consts_start, consts_arrived, consts_sent = copy_all(mine_c, gathered_c, send_g, recv_g)

    all_directions(copy_coef, 1, lambda c: c.start())
    all_directions(copy_tops, 1, lambda c: c.start())
    load_source.wait()
    all_directions(copy_source, 1, lambda c: c.start())

    slot = lax.broadcasted_iota(jnp.int32, (by2, depth), 1) % 4
    pick2 = selector(by2, 0, 4, depth)
    first_slot = lax.rem(w * bx2, 4)
    consts = jnp.zeros((by2, depth), jnp.float32)
    for x in range(bx2):
        coef = None
        for r in range(2):
            a = HALO + 1 + 4 * x + 2 * r
            pair = fine[1, a, HALO:HALO + by] + fine[1, a + 1, HALO:HALO + by]
            pair = pair_rows(pair_lanes(pair, 1, add), pool_g, 2 * x + r, add) * 0.125
            coef = pair if coef is None else coef + pair
        coef = pair_rows(pair_lanes(coef, 2, add), pool_h, x, add) * 0.125
        top = jnp.max(tops[4, 4 * x:4 * x + 4], axis=0, keepdims=True)
        top = jnp.maximum(top, pltpu.roll(top, depth - 1, 1))
        top = jnp.maximum(top, pltpu.roll(top, depth - 2, 1))
        here = first_slot + x
        consts = jnp.where(slot == here, coef, consts)
        consts = jnp.where(slot == lax.rem(here + 2, 4), column(pick2, top), consts)
    mine_c[...] = consts
    consts_start()
    gathered_c[me] = mine_c[...]

    all_directions(copy_tops, -1, lambda c: c.wait_recv())
    reach = HALO - 2
    picks = (selector(HALO, by - HALO, 1, depth), selector(by, 0, 1, depth),
             selector(HALO, 0, 1, depth))
    starts = (0, HALO, HALO + by)
    for x in range(HALO - reach, HALO + bx + reach):
        row = x - HALO + bx
        for k in range(3):
            line = tops[row // bx * 3 + k, row % bx:row % bx + 1]
            f_top[x, starts[k]:starts[k] + picks[k].shape[0]] = column(picks[k], line)
    pick1 = selector(by1, 0, 2, depth)
    for x in range(1, xo - 1):
        row = 2 * (x - 1)
        for k in range(3):
            line = jnp.max(tops[row // bx * 3 + k, row % bx:row % bx + 2], axis=0, keepdims=True)
            line = jnp.maximum(line, pltpu.roll(line, depth - 1, 1))
            o_top[x, k * by1:(k + 1) * by1] = column(pick1, line)

    all_directions(copy_coef, -1, lambda c: c.wait_recv())
    level0 = Level(x0, y0, depth, 1, *fw)
    level0.setup(lambda x: fine[1, x + 1], lambda x: f_top[x], HALO - reach, HALO + bx + reach)

    def coef1(x):
        coef = fine[1, 2 * x + 1] + fine[1, 2 * x + 2]
        m_coef[x + 1] = pair_rows(pair_lanes(coef, 1, add), pool_b, x, add) * 0.125

    planes(half - 3, half + bx1 + 3, coef1)
    level1 = Level(x1, y1, depth, 2, *mw)
    level1.setup(lambda x: m_coef[x + 1], lambda x: o_top[x + ring - half, by1 - half:by1 - half + y1],
                 half - 2, half + bx1 + 2)

    all_directions(copy_source, -1, lambda c: c.wait_recv())

    def load0(x):
        f_load[x] = level0.act[x] * fine[0, x + 1]

    planes(HALO - reach, HALO + bx + reach, load0)
    level0.smooth_fresh(f_load, f_u, f_smooth, HALO - reach, HALO + bx + reach)

    def restrict0(x):
        a, b = 2 * x, 2 * x + 1
        rest = (f_load[a] - level0.apply(f_smooth, a)) + (f_load[b] - level0.apply(f_smooth, b))
        m_load[x] = pair_rows(pair_lanes(rest, 1, add), pool_a, x, add)

    planes(half - 2, half + bx1 + 2, restrict0)

    even = lax.broadcasted_iota(jnp.int32, (by1, depth), 1) % 2 == 0
    for r in range(bx1 + 2):
        x = half - 1 + r
        packed[r] = jnp.where(even, m_load[x, half:half + by1], m_coef[x + 1, half:half + by1])
    all_directions(copy_outer, 1, lambda c: c.start())
    for r in range(bx1):
        outer[ring + r, by1:2 * by1] = packed[r + 1]

    level1.smooth_fresh(m_load, m_u, m_smooth, half - 2, half + bx1 + 2)
    rows = by2 // 2
    loads = jnp.zeros((rows, depth), jnp.float32)
    for x in range(bx2):
        a, b = half + 2 * x, half + 2 * x + 1
        rest = (m_load[a] - level1.apply(m_smooth, a)) + (m_load[b] - level1.apply(m_smooth, b))
        load = pair_rows(pair_lanes(rest, 2, add), pool_d, x, add)
        here = first_slot + x
        loads = jnp.where(slot[:rows] == here, load[quarter:quarter + rows], loads)
        loads = jnp.where(slot[:rows] == lax.rem(here + 2, 4),
                          load[quarter + rows:quarter + by2], loads)
    mine[...] = loads

    coarse_start()
    gathered[me] = mine[...]

    consts_arrived()

    def unpair(places, x, k):
        near, far = places[2 * x * grp + k], places[(2 * x + 1) * grp + k]
        lower = slot[:near.shape[0]] < 2
        return (jnp.where(lower, near, far),
                jnp.where(lower, pltpu.roll(near, depth - 2, 1), pltpu.roll(far, 2, 1)))

    def unpack_consts(x):
        for k in range(grp):
            own = pl.ds(k * by2, by2)
            g_coef[x + 1, own], g_top[x, own] = unpair(gathered_c, x, k)

    nq = nx2 // 4
    planes(0, nq, unpack_consts)
    level2 = Coarse(nq, ny2, depth, *gw)
    level2.setup(g_coef, g_top)
    zero = jnp.zeros((ny2, depth), jnp.float32)

    def reset(x):
        g_p[x] = zero
        g_s[x] = zero
        sol[x + 1] = zero

    planes(0, nq, reset)

    all_directions(copy_outer, -1, lambda c: c.wait_recv())

    def unpack1(x):
        both = outer[x]
        o_load[x] = keep_lane(both, 0, 2)
        o_coef[x + 1] = keep_lane(both, 1, 2)

    planes(0, xo, unpack1)
    level_o = Level(xo, yo, depth, 2, *ow)
    level_o.setup(lambda x: o_coef[x + 1], lambda x: o_top[x], 1, xo - 1)
    level_o.smooth_fresh(o_load, o_u, o_smooth, 1, xo - 1)

    coarse_arrived()

    def unpack_loads(x):
        for k in range(grp):
            low, high = unpair(gathered, x, k)
            g_r[x + 1, k * by2:k * by2 + rows] = low
            g_r[x + 1, k * by2 + rows:(k + 1) * by2] = high

    planes(0, nq, unpack_loads)

    def total(values):
        return jnp.sum(values, axis=(0, 1), keepdims=True)

    def iterate(_, carry):
        before, step_before = carry

        def image(x, sums):
            here, applied = level2.apply(g_r, x)
            g_a[x] = applied
            return sums[0] + here * here, sums[1] + here * applied

        squares, products = planes(0, nq, image, (zero, zero))
        current, curvature = total(squares), total(products)
        ratio = current / before
        step = current / (curvature - ratio * current / step_before)

        def move(x):
            direction = g_r[x + 1] + ratio * g_p[x]
            applied = g_a[x] + ratio * g_s[x]
            g_p[x], g_s[x] = direction, applied
            sol[x + 1] = sol[x + 1] + step * direction
            g_r[x + 1] = g_r[x + 1] - step * applied

        planes(0, nq, move)
        return current, step

    one = jnp.ones((1, 1), jnp.float32)
    lax.fori_loop(0, ITERS, iterate, (one * jnp.inf, one))

    spans = range((2 - ring) // 2, (xo - 3 - ring) // 2 + 1)
    slot2 = level2.slot
    for p in spans:
        x = w * bx2 + p + 4
        kept = jnp.where(slot2 == lax.rem(x, 4), sol[x // 4], 0.0)
        kept = pair_lanes(pair_lanes(kept, 1, add), 2, add)
        for k in range(grp):
            g_x[p - spans[0], k + 1] = kept[k * by2:(k + 1) * by2]

    for x in range(2, xo - 2):
        parent = (x - ring) // 2
        for k in range(3):
            piece = g_x[parent - spans[0], g + k]
            wide_rows[x, pl.ds(k * by1, by2, stride=2)] = piece
            wide_rows[x, pl.ds(k * by1 + 1, by2, stride=2)] = piece
        o_corr[x + 1] = o_smooth[x + 1] + level_o.act[x] * wide_rows[x]

    def put_outer(x, value):
        o_load[x] = value

    level_o.smooth_again(o_corr, o_load, o_e, o_u, ring - 1, ring + bx1 + 1, put_outer)

    for x in range(HALO - 2, HALO + bx + 2):
        parent = o_load[(x - HALO) // 2 + ring, by1 - half:2 * by1 + half]
        fine_rows[x, pl.ds(0, y1, stride=2)] = parent
        fine_rows[x, pl.ds(1, y1, stride=2)] = parent
        f_smooth[x + 1] = f_smooth[x + 1] + level0.act[x] * fine_rows[x]

    def copy_out(x):
        return pltpu.make_async_copy(result.at[x], out.at[x], sem_out.at[x])

    def put_fine(x, value):
        result[x - HALO] = value[HALO:HALO + by]
        copy_out(x - HALO).start()

    level0.smooth_again(f_smooth, f_load, f_e, f_u, HALO, HALO + bx, put_fine)

    for make in (copy_coef, copy_tops, copy_source, copy_outer):
        all_directions(make, 1, lambda c: c.wait_send())
    consts_sent()
    coarse_sent()
    planes(0, bx, lambda x: copy_out(x).wait())


def shards(source, conductivity, ice_cells):
    wide, grp = lax.axis_size("wide"), lax.axis_size("grp")
    bx, by, depth = source.shape
    bx1, by1, bx2, by2 = bx // 2, by // 2, bx // 4, by // 4
    x0, y0 = bx + 2 * HALO, by + 2 * HALO
    x1, y1 = x0 // 2, y0 // 2
    ring = bx1 + 1
    xo, yo = bx1 + 2 * ring, 3 * by1
    nq, ny2 = wide * bx2 // 4, grp * by2
    peers = wide * grp

    def block(*shape):
        return pltpu.VMEM(shape + (depth,), jnp.float32)

    def held(count, width):
        return [block(count + 1, width)] + [block(count, width) for _ in range(7)]

    dma = pltpu.SemaphoreType.DMA
    scratch = [
        block(2, x0 + 2, y0), held(x0, y0), block(x0, y0), block(x0 + 2, y0), block(x0 + 2, y0),
        block(x0, y0), block(x0, y0), block(x1, y0), block(x1, y0),
        block(x1, y1), block(x1 + 2, y1), held(x1, y1), block(x1 + 2, y1),
        block(x1 + 2, y1), block(bx1 + 2, by1),
        block(xo, yo), block(xo, yo), block(xo + 2, yo), block(xo, yo), held(xo, yo),
        block(xo + 2, yo), block(xo + 2, yo), block(xo, yo), block(xo + 2, yo),
        block(bx2, y1), block(bx1, by), block(bx2, by1), block(by2 // 2), block(by2),
        block(peers, by2 // 2), block(peers, by2),
        block(nq + 2, ny2), block(nq, ny2), [block(nq, ny2) for _ in range(8)],
        block(xo // 2, grp + 2, by2), block(nq + 2, ny2), block(nq, ny2), block(nq, ny2),
        block(nq, ny2), block(nq + 2, ny2),
        block(xo, yo), block(x0, y0),
        block(9, bx), pltpu.VMEM((bx, by), jnp.int32), block(bx, by), dma((3,)), dma((bx,)),
        *[dma((8,)) for _ in range(8)], *[dma((peers,)) for _ in range(4)],
    ]
    leaves, tree = jax.tree.flatten(scratch)

    def body(source_ref, conductivity_ref, ice_ref, out_ref, *refs):
        kernel(wide, grp, source_ref, conductivity_ref, ice_ref, out_ref,
               *jax.tree.unflatten(tree, refs))

    hbm = pl.BlockSpec(memory_space=pltpu.HBM)
    return pl.pallas_call(
        body,
        out_shape=jax.ShapeDtypeStruct(source.shape, source.dtype),
        in_specs=[hbm] * 3,
        out_specs=hbm,
        scratch_shapes=leaves,
        compiler_params=pltpu.CompilerParams(
            collective_id=0, has_side_effects=True, vmem_limit_bytes=64 * 1024 * 1024
        ),
    )(source, conductivity, ice_cells)


def solution(mesh):
    placed = (P("wide", "grp", None), P("wide", "grp", None), P("wide", "grp"))
    return jax.shard_map(
        shards, mesh=mesh, in_specs=placed, out_specs=P("wide", "grp", None), check_vma=False
    )
```
